32 devices in a mesh: groups: 2 (over y), seq: 16 (over z, x, core).
Axes of the slice: x: 2, y: 2, z: 4, core: 2. Of those that a mesh axis runs over, the one named last changes fastest.
Arguments:
- queries: bfloat16 [4096, 4096], P(('groups', 'seq')), parts along dimension 0, may hold values from -6 to 6
- suffix_kv: bfloat16 [4096, 1024], P(('groups', 'seq')), parts along dimension 0, may hold values from -6 to 6
- kv_store: bfloat16 [1024, 8, 1024], P(('groups', 'seq')), parts along dimension 0, may hold values from -6 to 6
- page_table: int32 [4, 16], P('groups'), parts along dimension 0, may hold values from 0 to 511, as said below
- hit_tokens: int32 [4], P('groups'), parts along dimension 0, may hold values from 0 to 128, as said below
- owner_offset: int32 [4, 4], P('groups'), parts along dimension 0, may hold values from 0 to 15
Outputs:
- attention_out: bfloat16 [4096, 4096], P(('groups', 'seq')), parts along dimension 0
- decode_cache: bfloat16 [32, 4, 128, 256], P(('groups', 'seq')), parts along dimension 0
The draws below stay inside these ranges and needn't reach their ends.
There are 2 independent parts, one for each index of `groups`. The reference program is written for one: setup_inputs(seed, part) draws one part's arguments, and reference() takes and returns one part's arrays. A program takes and returns all parts, laid end to end along the dimension named above; each array names one. Nothing has to cross between parts.
Inputs may be any that keep to these rules, and one draw needn't show every extreme that they name: Slot page_table[r, j] is slot page_table[r, j] mod 32 of store device page_table[r, j] // 32; all entries of one group differ, and every store device holds exactly 1 pages of each request. `hit_tokens`: some request finds all 128 prefix tokens.
All inputs are finite; a program needn't handle non-finite values.
Results may differ from the reference program's by a relative error of at most 0.007.
Values may be sent and summed in bfloat16 or wider, within the bound.
No kernel may reach another device: no remote copies, remote signals or barrier semaphores. Data moves between devices by JAX's collectives and lax.ppermute only.
A program may use at most 128 MiB of HBM per device.

```python
from functools import partial
import jax
import jax.numpy as jnp
from jax import lax

HD = 128
QH = 32
KVH = 4
REQS = 2
TOK_DEV = 128
PAGE = 8
CAP = 1
SLOTS = 32
TOKENS = 2048
MAXP = 16
N_SEQ = 16


def shuffle_rows(keys_in, count):
    return jax.vmap(partial(jax.random.permutation, x=count))(keys_in)


def draw_queries(key, part):
    key = jax.random.fold_in(key, 11)
    drawn = jnp.clip(jax.random.normal(key, (TOKENS, QH, HD)), -6.0, 6.0)
    return drawn.reshape(TOKENS, QH * HD).astype(jnp.bfloat16)


def draw_suffix_kv(key, part):
    key = jax.random.fold_in(key, 12)
    drawn = jnp.clip(jax.random.normal(key, (TOKENS, KVH, 2, HD)), -6.0, 6.0)
    return drawn.reshape(TOKENS, KVH * 2 * HD).astype(jnp.bfloat16)


def draw_page_table(key, part):
    key = jax.random.fold_in(key, 13)
    spread_key, slot_key = jax.random.split(key)
    spread = shuffle_rows(jax.random.split(spread_key, REQS), N_SEQ * CAP)[:, :MAXP]
    store_index = spread // CAP
    slot_rank = spread % CAP
    slot_order = shuffle_rows(jax.random.split(slot_key, N_SEQ), SLOTS)
    wanted = jnp.arange(REQS, dtype=jnp.int32)[:, None] * CAP + slot_rank
    local_slot = slot_order[store_index, wanted]
    return (store_index * SLOTS + local_slot).astype(jnp.int32)


def draw_hit_tokens(key, part):
    key = jax.random.fold_in(key, 14)
    first_key, second_key = jax.random.split(key)
    most = MAXP * PAGE
    uniform_hits = jax.random.randint(first_key, (REQS,), 0, most + 1)
    skewed = uniform_hits * uniform_hits // most
    full_request = jax.random.randint(second_key, (), 0, REQS)
    return jnp.where(jnp.arange(REQS, dtype=jnp.int32) == full_request, most, skewed).astype(jnp.int32)


def set_ends(values, stream_key, low, largest):
    longest = values.shape.index(max(values.shape))
    spots = []
    for shift in (0, 1):
        where = [jax.random.randint(jax.random.fold_in(stream_key, axis), (), 0, length) for axis, length in enumerate(values.shape)]
        where[longest] = (where[longest] + shift) % values.shape[longest]
        spots.append(tuple(where))
    return values.at[spots[0]].set(low).at[spots[1]].set(largest)


def levels(own_key, dims, cuts, least, largest):
    def one(dim, shards_of):
        draws = jax.random.uniform(jax.random.fold_in(jax.random.fold_in(own_key, 6), dim), (shards_of,), jnp.float32, least / len(cuts), largest / len(cuts))
        return jnp.repeat(jnp.exp(draws), dims[dim] // shards_of).reshape((-1,) + (1,) * (len(dims) - dim - 1))

    gain = one(*cuts[0])
    for cut in cuts[1:]:
        gain = gain * one(*cut)
    return gain


def bell_draw(rng, dims, scale, most, cuts=(), kind=jnp.bfloat16):
    factor_of = levels(rng, dims, cuts, -0.22, 0.18) if cuts else 1.0
    entries = jax.random.normal(rng, dims, jnp.float32) * scale * factor_of
    return jnp.minimum(jnp.maximum(entries, -most), most).astype(kind)


def setup_inputs(seed: int = 0, part: int = 0) -> dict:
    key_of = jax.random.split(jax.random.key(seed), 7)
    part_splits = jax.random.split(jax.random.fold_in(key_of[6], part), 7)
    queries = draw_queries(jax.random.fold_in(jax.random.fold_in(key_of[6], part), 71), part)
    suffix_kv = draw_suffix_kv(jax.random.fold_in(jax.random.fold_in(key_of[6], part), 71), part)
    kv_store = bell_draw(part_splits[2], (N_SEQ * SLOTS, PAGE, KVH * 2 * HD), 1.0, 6.0, ((0, 16),))
    page_table = draw_page_table(jax.random.fold_in(jax.random.fold_in(key_of[6], part), 71), part)
    hit_tokens = draw_hit_tokens(jax.random.fold_in(jax.random.fold_in(key_of[6], part), 71), part)
    owner_offset = set_ends(jax.random.randint(part_splits[5], (REQS, KVH), 0, N_SEQ), jax.random.fold_in(part_splits[5], 1), 0, N_SEQ - 1).astype(jnp.int32)
    return {"queries": queries, "suffix_kv": suffix_kv, "kv_store": kv_store, "page_table": page_table, "hit_tokens": hit_tokens, "owner_offset": owner_offset}


def reference(queries, suffix_kv, kv_store, page_table, hit_tokens, owner_offset):
    group_size = N_SEQ // REQS
    per_group = QH // KVH
    suffix_len = TOK_DEV * group_size
    prefix_len = N_SEQ * CAP * PAGE
    score_scale = HD ** -0.5

    def one_block(block_id):
        request = block_id // group_size
        rank_in_group = block_id % group_size
        query_rows = lax.dynamic_slice_in_dim(queries, block_id * TOK_DEV, TOK_DEV, 0)
        query_rows = query_rows.reshape(TOK_DEV, KVH, per_group, HD).astype(jnp.float32)
        prefix_pages = kv_store[page_table[request]].reshape(prefix_len, KVH, 2 * HD)
        suffix_rows = lax.dynamic_slice_in_dim(suffix_kv, request * suffix_len, suffix_len, 0)
        suffix_rows = suffix_rows.reshape(suffix_len, KVH, 2 * HD)
        all_keys = jnp.concatenate([prefix_pages, suffix_rows], axis=0).astype(jnp.float32)
        prefix_ok = jnp.arange(prefix_len, dtype=jnp.int32) < hit_tokens[request]
        query_pos = rank_in_group * TOK_DEV + jnp.arange(TOK_DEV, dtype=jnp.int32)
        suffix_ok = jnp.arange(suffix_len, dtype=jnp.int32)[None, :] <= query_pos[:, None]
        usable = jnp.concatenate([jnp.broadcast_to(prefix_ok[None, :], (TOK_DEV, prefix_len)), suffix_ok], axis=1)
        scores = jnp.einsum("tgqd,kgd->gtqk", query_rows, all_keys[:, :, :HD]) * score_scale
        scores = jnp.where(usable[None, :, None, :], scores, -jnp.inf)
        top_score = jnp.max(scores, axis=-1, keepdims=True)
        probabilities = jnp.exp(scores - top_score)
        denominator = jnp.sum(probabilities, axis=-1)
        rounded = probabilities.astype(jnp.bfloat16).astype(jnp.float32)
        weighted = jnp.einsum("gtqk,kgd->gtqd", rounded, all_keys[:, :, HD:])
        result = (weighted / denominator[..., None]).astype(jnp.bfloat16)
        return result.transpose(1, 0, 2, 3).reshape(TOK_DEV, QH * HD)

    attention_out = lax.map(one_block, jnp.arange(N_SEQ, dtype=jnp.int32)).reshape(N_SEQ * TOK_DEV, QH * HD)

    stacked = suffix_kv.reshape(REQS, suffix_len // N_SEQ, N_SEQ, KVH, 2 * HD).transpose(0, 3, 2, 1, 4)
    owners = jnp.arange(N_SEQ, dtype=jnp.int32)
    columns = (owners[None, None, :] - owner_offset[:, :, None]) % N_SEQ
    placed = jnp.take_along_axis(stacked, columns[:, :, :, None, None], axis=2)
    decode_cache = placed.transpose(2, 1, 0, 3, 4).reshape(N_SEQ, KVH, REQS * (suffix_len // N_SEQ), 2 * HD)
    return attention_out, decode_cache
```

```python
import functools

import jax
import jax.numpy as jnp
from jax import lax
from jax.experimental import pallas as pl
from jax.experimental.pallas import tpu as pltpu
from jax.sharding import PartitionSpec as P

HD = 128
QH = 32
KVH = 4
REQS = 2
PAGE = 8
SLOTS = 32
GQ = QH // KVH

LOG2E = 1.4426950408889634
OUT_OF_REACH = -1e30
CHUNK = 384
VMEM_BYTES = 48 * 1024 * 1024
CONTRACT_LAST = (((1,), (1,)), ((), ()))

IN_VMEM = pl.BlockSpec(memory_space=pltpu.VMEM)
IN_SMEM = pl.BlockSpec(memory_space=pltpu.SMEM)
ANYWHERE = pl.BlockSpec(memory_space=pl.ANY)


def hop_bits(devices):
    bits = []
    bit = 2
    while bit < devices // REQS:
        bits.append(bit)
        bit *= 2
    return (tuple(bits), tuple(reversed(bits)))


def pick(core, pair):
    return jnp.where(core == 0, pair[0], pair[1])


def swap(value, bit):
    route = [(i, i ^ bit) for i in range(lax.axis_size("seq"))]
    return lax.ppermute(value, "seq", route)


def swap_by_core(value, orders, step):
    route = [(i, i ^ orders[i % 2][step]) for i in range(lax.axis_size("seq"))]
    return lax.ppermute(value, "seq", route)


def page_kernel(devices, table_ref, store_ref, own_ref, other_ref, sems):
    me = lax.axis_index("seq")
    request = me // (devices // REQS)

    def slot_of(req):
        def visit(j, found):
            entry = table_ref[req, j]
            return jnp.where(entry // SLOTS == me, entry % SLOTS, found)

        return lax.fori_loop(0, table_ref.shape[1], visit, jnp.int32(0), unroll=True)

    other = pltpu.make_async_copy(store_ref.at[slot_of(1 - request)], other_ref, sems.at[0])
    other.start()
    own = pltpu.make_async_copy(store_ref.at[slot_of(request)], own_ref, sems.at[1])
    own.start()
    other.wait()
    own.wait()


def fetch_pages(page_table, kv_store, devices):
    page = jax.ShapeDtypeStruct(kv_store.shape[1:], kv_store.dtype)
    return pl.pallas_call(
        functools.partial(page_kernel, devices),
        out_shape=(page, page),
        in_specs=[IN_SMEM, ANYWHERE],
        out_specs=(ANYWHERE, ANYWHERE),
        scratch_shapes=[pltpu.SemaphoreType.DMA((2,))],
        name="fetch_pages",
    )(page_table, kv_store)


def source_of(me, swapped, steps, orders):
    at = me ^ 1 if swapped else me
    core = at % 2
    for step in steps:
        at = at ^ pick(core, (orders[0][step], orders[1][step]))
    return at


def prefix_bias(me, devices, orders, table_ref, hit_ref, swapped, rows):
    lane = lax.broadcasted_iota(jnp.int32, (1, rows), 1)
    slot = lane // PAGE
    at = jnp.full((1, rows), me ^ 1 if swapped else me, jnp.int32)
    core = (me ^ 1 if swapped else me) % 2
    hops = [devices // REQS] + [pick(core, (orders[0][s], orders[1][s])) for s in range(len(orders[0]))]
    for n, hop in enumerate(hops):
        at = jnp.where((slot // (2**n)) % 2 == 1, at ^ hop, at)
    request = me // (devices // REQS)

    def visit(j, page):
        return jnp.where(at == table_ref[request, j] // SLOTS, j, page)

    page = lax.fori_loop(0, table_ref.shape[1], visit, jnp.zeros((1, rows), jnp.int32), unroll=True)
    return jnp.where(page * PAGE + lane % PAGE < hit_ref[request], 0.0, OUT_OF_REACH)


def attend_kernel(devices, orders, kinds, first, last, *refs):
    refs = list(refs)
    table_ref, hit_ref, q_ref = refs[:3]
    key_refs = refs[3 : 3 + len(kinds)]
    rest = refs[3 + len(kinds) :]
    if not first:
        top_in, denom_in, sum_in = rest[:3]
        rest = rest[3:]
    if last:
        (out_ref,) = rest
    else:
        top_ref, denom_ref, sum_ref = rest
    me = lax.axis_index("seq")
    rows = q_ref.shape[0]

    pieces = []
    for ref, kind in zip(key_refs, kinds):
        length = ref.shape[0]
        if kind[0] == "own":
            t = lax.broadcasted_iota(jnp.int32, (rows, length), 0)
            k = lax.broadcasted_iota(jnp.int32, (rows, length), 1)
            bias = jnp.where(k <= t, 0.0, OUT_OF_REACH)
        elif kind[0] == "block":
            source = source_of(me, kind[1], kind[2], orders)
            bias = jnp.full((1, length), jnp.where(source < me, 0.0, OUT_OF_REACH), jnp.float32)
        else:
            bias = prefix_bias(me, devices, orders, table_ref, hit_ref, kind[1], length)
        for at in range(0, length, 128):
            size = min(128, length - at)
            pieces.append((ref, at, size, bias[:, at : at + size]))
    chunks = []
    for piece in pieces:
        if chunks and sum(p[2] for p in chunks[-1]) + piece[2] <= CHUNK:
            chunks[-1].append(piece)
        else:
            chunks.append([piece])

    full_biases = []
    for chunk in chunks:
        tall = any(p[3].shape[0] > 1 for p in chunk)
        full_biases.append(
            jnp.concatenate([jnp.broadcast_to(p[3], (rows if tall else 1, p[2])) for p in chunk], axis=1)
        )

    scale = HD**-0.5 * LOG2E
    for g in range(KVH):
        heads = range(g * GQ, (g + 1) * GQ)
        span = pl.ds(g * GQ * rows, GQ * rows)
        q = jnp.concatenate([q_ref[:, h * HD : (h + 1) * HD] for h in heads], axis=0)
        top = denom = total = None
        if not first:
            top, denom, total = top_in[span, 0:1], denom_in[span, 0:1], sum_in[span, :]
        for chunk, bias in zip(chunks, full_biases):
            at = g * 2 * HD
            keys = jnp.concatenate([p[0][p[1] : p[1] + p[2], at : at + HD] for p in chunk], axis=0)
            values = jnp.concatenate([p[0][p[1] : p[1] + p[2], at + HD : at + 2 * HD] for p in chunk], axis=0)
            scores = lax.dot_general(q, keys, CONTRACT_LAST, preferred_element_type=jnp.float32)
            if bias.shape[0] > 1:
                scores = (scores.reshape(GQ, rows, -1) + bias[None]).reshape(GQ * rows, -1)
            else:
                scores = scores + bias
            peak = jnp.max(scores, axis=1, keepdims=True)
            new_top = peak if top is None else jnp.maximum(top, peak)
            probabilities = jnp.exp2((scores - new_top) * scale)
            mass = jnp.sum(probabilities, axis=1, keepdims=True)
            weighted = jnp.dot(probabilities.astype(jnp.bfloat16), values, preferred_element_type=jnp.float32)
            if top is None:
                denom, total = mass, weighted
            else:
                factor = jnp.exp2((top - new_top) * scale)
                denom, total = denom * factor + mass, total * factor + weighted
            top = new_top
        if last:
            attended = (total / denom).astype(out_ref.dtype)
            for n, h in enumerate(heads):
                out_ref[:, h * HD : (h + 1) * HD] = attended[n * rows : (n + 1) * rows]
        else:
            top_ref[span, :] = jnp.broadcast_to(top, (GQ * rows, HD))
            denom_ref[span, :] = jnp.broadcast_to(denom, (GQ * rows, HD))
            sum_ref[span, :] = total


def attend(devices, orders, page_table, hit_tokens, queries, arrays, kinds, running, last):
    rows = queries.shape[0]
    count = len(arrays)
    keys = sum(a.shape[0] for a in arrays)
    if last:
        out_shape = jax.ShapeDtypeStruct((rows, QH * HD), queries.dtype)
        out_specs = IN_VMEM
    else:
        out_shape = (jax.ShapeDtypeStruct((QH * rows, HD), jnp.float32),) * 3
        out_specs = (IN_VMEM,) * 3
    state = () if running is None else tuple(running)
    return pl.pallas_call(
        functools.partial(attend_kernel, devices, orders, tuple(kinds), running is None, last),
        out_shape=out_shape,
        in_specs=[IN_SMEM, IN_SMEM, IN_VMEM] + [IN_VMEM] * (count + len(state)),
        out_specs=out_specs,
        input_output_aliases={} if last or not state else {3 + count + n: n for n in range(3)},
        compiler_params=pltpu.CompilerParams(vmem_limit_bytes=VMEM_BYTES),
        cost_estimate=pl.CostEstimate(
            flops=8 * rows * QH * keys * HD, bytes_accessed=4 * rows * QH * HD, transcendentals=rows * QH * keys
        ),
        name="attend",
    )(page_table, hit_tokens, queries, *arrays, *state)


def owner_kernel(devices, orders, kinds, offset_ref, *refs):
    key_refs = refs[: len(kinds)]
    own_ref, other_ref = refs[len(kinds) :]
    me = lax.axis_index("seq")
    group_size = devices // REQS
    request = me // group_size
    rows = key_refs[0].shape[0]
    kept = own_ref.shape[1]
    targets = []
    row = lax.broadcasted_iota(jnp.int32, (2 * kept, rows), 0)
    lane = lax.broadcasted_iota(jnp.int32, (1, rows), 1)
    half = row >= kept
    for ref, kind in zip(key_refs, kinds):
        source = me if kind[0] == "own" else source_of(me, kind[1], kind[2], orders)
        position = (source % group_size) * rows + lane
        targets.append(position)
    for g in range(KVH):
        turn = (me - offset_ref[request, g] + devices) % devices
        other_turn = turn ^ (devices // REQS)
        total = jnp.zeros((2 * kept, 2 * HD), jnp.float32)
        for ref, position in zip(key_refs, targets):
            m, residue = position // devices, position % devices
            chosen = (jnp.where(half, other_turn, turn) == residue) & (jnp.where(half, row - kept, row) == m)
            total = total + jnp.dot(
                jnp.where(chosen, 1.0, 0.0).astype(jnp.bfloat16),
                ref[:, g * 2 * HD : (g + 1) * 2 * HD],
                preferred_element_type=jnp.float32,
            )
        own_ref[g] = total[:kept].astype(own_ref.dtype)
        other_ref[g] = total[kept:].astype(other_ref.dtype)


def pick_for_owners(devices, orders, owner_offset, arrays, kinds):
    rows, width = arrays[0].shape
    kept = (devices // REQS) * rows // devices
    piece = jax.ShapeDtypeStruct((KVH, kept, 2 * HD), arrays[0].dtype)
    return pl.pallas_call(
        functools.partial(owner_kernel, devices, orders, tuple(kinds)),
        out_shape=(piece, piece),
        in_specs=[IN_SMEM] + [IN_VMEM] * len(arrays),
        out_specs=(IN_VMEM, IN_VMEM),
        compiler_params=pltpu.CompilerParams(vmem_limit_bytes=VMEM_BYTES),
        name="pick_for_owners",
    )(owner_offset, *arrays)


def place_kernel(devices, own_ref, other_ref, out_ref):
    request = lax.axis_index("seq") // (devices // REQS)
    kept = own_ref.shape[1]

    @pl.when(request == 0)
    def _():
        out_ref[0, :, :kept] = own_ref[...]
        out_ref[0, :, kept:] = other_ref[...]

    @pl.when(request == 1)
    def _():
        out_ref[0, :, :kept] = other_ref[...]
        out_ref[0, :, kept:] = own_ref[...]


def place(devices, own, other):
    heads, kept, width = own.shape
    return pl.pallas_call(
        functools.partial(place_kernel, devices),
        out_shape=jax.ShapeDtypeStruct((1, heads, REQS * kept, width), own.dtype),
        in_specs=[IN_VMEM, IN_VMEM],
        out_specs=IN_VMEM,
        name="place",
    )(own, other)


def shards(queries, suffix_kv, kv_store, page_table, hit_tokens, owner_offset):
    devices = lax.axis_size("seq")
    orders = hop_bits(devices)
    steps = len(orders[0])

    held = [((), suffix_kv)]
    moved = []
    for step in range(steps):
        arrived = [(path + (step,), swap_by_core(value, orders, step)) for path, value in held]
        moved.append(arrived)
        held = held + arrived
    own_swapped = swap(suffix_kv, 1)
    moved_swapped = [[(path, swap(value, 1)) for path, value in arrived] for arrived in moved]

    own_page, other_page = fetch_pages(page_table, kv_store, devices)
    pages = jnp.concatenate([own_page, swap(other_page, devices // REQS)], axis=0)
    for step in range(steps):
        pages = jnp.concatenate([pages, swap_by_core(pages, orders, step)], axis=0)
    pages_swapped = swap(pages, 1)

    call = functools.partial(attend, devices, orders, page_table, hit_tokens, queries)
    running = call([suffix_kv, own_swapped], [("own",), ("block", True, ())], None, False)
    arrays, kinds = [], []
    batches = []
    for step in range(steps):
        for (path, value), (_, value_swapped) in zip(reversed(moved[step]), reversed(moved_swapped[step])):
            batches.append(([value, value_swapped], [("block", False, path), ("block", True, path)]))
    everything = [suffix_kv, own_swapped]
    every_kind = [("own",), ("block", True, ())]
    for batch, batch_kinds in batches:
        everything += batch
        every_kind += batch_kinds
    own_piece, other_piece = pick_for_owners(devices, orders, owner_offset, everything, every_kind)
    landed = swap(other_piece, devices // REQS)

    for batch, batch_kinds in batches[:-1]:
        running = call(batch, batch_kinds, running, False)
    batch, batch_kinds = batches[-1]
    attention_out = call(
        batch + [pages, pages_swapped], batch_kinds + [("pages", False), ("pages", True)], running, True
    )
    return (attention_out, place(devices, own_piece, landed))


def solution(mesh):
    in_specs = (
        P(("groups", "seq"), None),
        P(("groups", "seq"), None),
        P(("groups", "seq"), None, None),
        P("groups", None),
        P("groups"),
        P("groups", None),
    )
    out_specs = (P(("groups", "seq"), None), P(("groups", "seq"), None, None, None))
    return jax.shard_map(shards, mesh=mesh, in_specs=in_specs, out_specs=out_specs, check_vma=False)
```

```python
import functools

import jax
import jax.numpy as jnp
from jax import lax
from jax.experimental import pallas as pl
from jax.experimental.pallas import tpu as pltpu
from jax.sharding import PartitionSpec as P

HD = 128
QH = 32
KVH = 4
REQS = 2
PAGE = 8
SLOTS = 32
GQ = QH // KVH

LOG2E = 1.4426950408889634
OUT_OF_REACH = -1e30
CHUNK = 512
VMEM_BYTES = 16 * 1024 * 1024
SAFE_MASS = 1e36
CONTRACT_LAST = (((1,), (1,)), ((), ()))

IN_VMEM = pl.BlockSpec(memory_space=pltpu.VMEM)
IN_SMEM = pl.BlockSpec(memory_space=pltpu.SMEM)
ANYWHERE = pl.BlockSpec(memory_space=pl.ANY)


def hop_bits(devices):
    bits = []
    bit = 2
    while bit < devices // REQS:
        bits.append(bit)
        bit *= 2
    return (tuple(bits), tuple(reversed(bits)))


def pick(core, pair):
    return jnp.where(core == 0, pair[0], pair[1])


def swap(value, bit):
    route = [(i, i ^ bit) for i in range(lax.axis_size("seq"))]
    return lax.ppermute(value, "seq", route)


def swap_by_core(value, orders, step):
    route = [(i, i ^ orders[i % 2][step]) for i in range(lax.axis_size("seq"))]
    return lax.ppermute(value, "seq", route)


def swap_wide(value, orders, bit):
    route = [(i, i ^ bit ^ orders[i % 2][0]) for i in range(lax.axis_size("seq"))]
    return lax.ppermute(value, "seq", route)


def after(value, *earlier):
    return lax.optimization_barrier((value,) + earlier)[0]


def page_kernel(devices, table_ref, store_ref, own_ref, other_ref, sems):
    me = lax.axis_index("seq")
    request = me // (devices // REQS)
    copies = []
    for n, (req, page_ref) in enumerate(((1 - request, other_ref), (request, own_ref))):
        slot = jnp.int32(0)
        for j in range(table_ref.shape[1]):
            away = table_ref[req, j] - me * SLOTS
            slot = jnp.where((away >= 0) & (away < SLOTS), away, slot)
        copy = pltpu.make_async_copy(store_ref.at[slot], page_ref, sems.at[n])
        copy.start()
        copies.append(copy)
    for copy in copies:
        copy.wait()


def fetch_pages(page_table, kv_store, devices):
    page = jax.ShapeDtypeStruct(kv_store.shape[1:], kv_store.dtype)
    return pl.pallas_call(
        functools.partial(page_kernel, devices),
        out_shape=(page, page),
        in_specs=[IN_SMEM, ANYWHERE],
        out_specs=(IN_VMEM, IN_VMEM),
        scratch_shapes=[pltpu.SemaphoreType.DMA((2,))],
        name="fetch_pages",
    )(page_table, kv_store)


def source_of(me, swapped, path, orders):
    at = me ^ 1 if swapped else me
    core = at % 2
    for step in path:
        at = at ^ pick(core, (orders[0][step], orders[1][step]))
    return at


def page_bias(me, devices, orders, table_ref, hit_ref, swapped, path, place):
    base = source_of(me, swapped, path, orders)
    hop = pick(base % 2, (orders[0][0], orders[1][0]))
    slot = place // PAGE
    at = jnp.where(slot >= 2, base ^ hop, base)
    at = jnp.where(slot % 2 == 1, at ^ (devices // REQS), at)
    request = me // (devices // REQS)
    page = jnp.zeros_like(place)
    for j in range(table_ref.shape[1]):
        page = jnp.where(at == table_ref[request, j] // SLOTS, j, page)
    return jnp.where(page * PAGE + place % PAGE < hit_ref[request], 0.0, OUT_OF_REACH)


def key_bias(me, devices, orders, table_ref, hit_ref, kind, shape, dim):
    if kind[0] == "own":
        return jnp.zeros(shape, jnp.float32)
    if kind[0] == "block":
        source = source_of(me, kind[1], kind[2], orders)
        return jnp.full(shape, jnp.where(source < me, 0.0, OUT_OF_REACH), jnp.float32)
    place = lax.broadcasted_iota(jnp.int32, shape, dim)
    return page_bias(me, devices, orders, table_ref, hit_ref, kind[1], kind[2], place)


def stack(refs, at):
    return jnp.concatenate([ref[:, at : at + HD] for ref in refs], axis=0)


def head_rows(q_ref, g):
    heads = range(g * GQ, (g + 1) * GQ)
    return jnp.concatenate([q_ref[:, h * HD : (h + 1) * HD] for h in heads], axis=0)


def with_ones(values):
    return jnp.concatenate([values, jnp.ones_like(values)], axis=1)


def shift_lanes(shift):
    lane = lax.broadcasted_iota(jnp.int32, shift.shape, 1)
    return jnp.where(lane == 0, -shift, jnp.where(lane == 1, 1.0, 0.0)).astype(jnp.bfloat16)


def bias_lanes(bias):
    lane = lax.broadcasted_iota(jnp.int32, bias.shape, 1)
    return jnp.where(lane == 0, 1.0, jnp.where(lane == 1, bias, 0.0)).astype(jnp.bfloat16)


def causal_bias(rows):
    t = lax.broadcasted_iota(jnp.int32, (rows, rows), 0)
    k = lax.broadcasted_iota(jnp.int32, (rows, rows), 1)
    return jnp.where(k <= t, 0.0, OUT_OF_REACH)


SCALE = HD**-0.5 * LOG2E


def first_kernel(orders, q_ref, own_ref, mate_ref, mass_ref, shift_ref):
    me = lax.axis_index("seq")
    rows = q_ref.shape[0]
    mate_bias = jnp.where(me % 2 == 1, 0.0, OUT_OF_REACH)
    bias = jnp.concatenate([causal_bias(rows), jnp.full((rows, rows), mate_bias, jnp.float32)], axis=1)
    refs = (own_ref, mate_ref)
    for g in range(KVH):
        at = g * 2 * HD
        scores = lax.dot_general(head_rows(q_ref, g), stack(refs, at), CONTRACT_LAST, preferred_element_type=jnp.float32)
        scores = (scores.reshape(GQ, rows, -1) + bias[None]).reshape(GQ * rows, -1)
        peak = jnp.max(scores, axis=1, keepdims=True)
        shift = jnp.broadcast_to(peak, (GQ * rows, HD)).astype(jnp.bfloat16).astype(jnp.float32)
        weights = jnp.exp2((scores - jnp.concatenate([shift, shift], axis=1)) * SCALE).astype(jnp.bfloat16)
        span = pl.ds(g * GQ * rows, GQ * rows)
        mass_ref[span, :] = jnp.dot(weights, with_ones(stack(refs, at + HD)), preferred_element_type=jnp.float32)
        shift_ref[span, :] = shift_lanes(shift)


def attend_first(orders, queries, own, mate):
    rows = queries.shape[0]
    return pl.pallas_call(
        functools.partial(first_kernel, orders),
        out_shape=(
            jax.ShapeDtypeStruct((QH * rows, 2 * HD), jnp.float32),
            jax.ShapeDtypeStruct((QH * rows, HD), jnp.bfloat16),
        ),
        in_specs=[IN_VMEM] * 3,
        out_specs=(IN_VMEM, IN_VMEM),
        compiler_params=pltpu.CompilerParams(vmem_limit_bytes=VMEM_BYTES),
        cost_estimate=pl.CostEstimate(
            flops=16 * rows * QH * rows * HD, bytes_accessed=4 * rows * QH * HD, transcendentals=2 * rows * QH * rows
        ),
        name="attend_first",
    )(queries, own, mate)


def more_kernel(devices, orders, kinds, extra_kinds, *refs):
    refs = list(refs)
    table_ref, hit_ref, q_ref, shift_ref, mass_ref = refs[:5]
    key_refs = refs[5 : 5 + len(kinds)]
    if extra_kinds is None:
        out_ref = refs[-1]
    else:
        out_ref, wrong_ref, top_ref, denominator_ref, total_ref, block_ref, sem = refs[-7:]
    me = lax.axis_index("seq")
    rows = q_ref.shape[0]
    span_rows = GQ * rows

    def bias_of(kind, ref):
        shape = (ref.shape[0], HD)
        return bias_lanes(key_bias(me, devices, orders, table_ref, hit_ref, kind, shape, 0))

    def add_up(q_wide, group, bias, at):
        keys = jnp.concatenate([stack(group, at), bias], axis=1)
        scores = lax.dot_general(q_wide, keys, CONTRACT_LAST, preferred_element_type=jnp.float32)
        weights = jnp.exp2(scores * SCALE).astype(jnp.bfloat16)
        return jnp.dot(weights, with_ones(stack(group, at + HD)), preferred_element_type=jnp.float32)

    bias = jnp.concatenate([bias_of(kind, ref) for kind, ref in zip(kinds, key_refs)], axis=0)
    if extra_kinds is not None:
        wrong_ref[...] = jnp.zeros_like(wrong_ref)
    for g in range(KVH):
        span = pl.ds(g * span_rows, span_rows)
        q_wide = jnp.concatenate([head_rows(q_ref, g), shift_ref[span, :]], axis=1)
        mass = mass_ref[span, :] + add_up(q_wide, key_refs, bias, g * 2 * HD)
        if extra_kinds is None:
            out_ref[span, :] = mass
            continue
        total, denominator = mass[:, :HD], mass[:, HD:]
        good = jnp.where(denominator < SAFE_MASS, 0.0, 1.0)
        wrong_ref[...] = jnp.maximum(wrong_ref[...], jnp.max(good.reshape(-1, 8, HD), axis=0))
        attended = (total / denominator).astype(out_ref.dtype)
        for n in range(GQ):
            h = g * GQ + n
            out_ref[:, h * HD : (h + 1) * HD] = attended[n * rows : (n + 1) * rows]
    if extra_kinds is None:
        return

    @pl.when(jnp.max(wrong_ref[...]) > 0.0)
    def _():
        top_ref[...] = jnp.full_like(top_ref, OUT_OF_REACH)
        denominator_ref[...] = jnp.zeros_like(denominator_ref)
        total_ref[...] = jnp.zeros_like(total_ref)

        def take(kind, ref):
            bias = key_bias(me, devices, orders, table_ref, hit_ref, kind, (1, ref.shape[0]), 1)
            if kind[0] == "own":
                bias = causal_bias(rows)

            def one_head(h, carried):
                column = pl.ds(pl.multiple_of(h * HD, HD), HD)
                at = pl.multiple_of(h // GQ * 2 * HD, 2 * HD)
                span = pl.ds(pl.multiple_of(h * rows, rows), rows)
                scores = lax.dot_general(
                    q_ref[:, column], ref[:, pl.ds(at, HD)], CONTRACT_LAST, preferred_element_type=jnp.float32
                )
                scores = scores + bias
                top = top_ref[span, :]
                new_top = jnp.maximum(top, jnp.max(scores, axis=1, keepdims=True))
                weights = jnp.exp2((scores - new_top[:, : scores.shape[1]]) * SCALE)
                factor = jnp.exp2((top - new_top) * SCALE)
                top_ref[span, :] = new_top
                denominator_ref[span, :] = denominator_ref[span, :] * factor + jnp.sum(weights, axis=1, keepdims=True)
                total_ref[span, :] = total_ref[span, :] * factor + jnp.dot(
                    weights.astype(jnp.bfloat16), ref[:, pl.ds(at + HD, HD)], preferred_element_type=jnp.float32
                )
                return carried

            lax.fori_loop(0, QH, one_head, 0)

        for kind, ref in zip(extra_kinds, refs[5 + len(kinds) :]):
            copy = pltpu.make_async_copy(ref, block_ref, sem)
            copy.start()
            copy.wait()
            take(kind, block_ref)
        for kind, ref in zip(kinds, key_refs):
            take(kind, ref)

        def write(h, carried):
            span = pl.ds(pl.multiple_of(h * rows, rows), rows)
            attended = total_ref[span, :] / denominator_ref[span, :]
            out_ref[:, pl.ds(pl.multiple_of(h * HD, HD), HD)] = attended.astype(out_ref.dtype)
            return carried

        lax.fori_loop(0, QH, write, 0)


def attend_more(devices, orders, page_table, hit_tokens, queries, shift, mass, batch, extra):
    rows = queries.shape[0]
    keys = sum(value.shape[0] for _, value in batch)
    last = extra is not None
    if last:
        out_shape = jax.ShapeDtypeStruct((rows, QH * HD), queries.dtype)
    else:
        out_shape = jax.ShapeDtypeStruct(mass.shape, mass.dtype)
    arrays = [value for _, value in batch] + [value for _, value in extra or ()]
    scratch = [
        pltpu.VMEM((8, HD), jnp.float32),
        *[pltpu.VMEM((QH * rows, HD), jnp.float32)] * 3,
        pltpu.VMEM((rows, 2 * KVH * HD), jnp.bfloat16),
        pltpu.SemaphoreType.DMA,
    ]
    return pl.pallas_call(
        functools.partial(
            more_kernel,
            devices,
            orders,
            tuple(kind for kind, _ in batch),
            tuple(kind for kind, _ in extra) if last else None,
        ),
        out_shape=out_shape,
        in_specs=[IN_SMEM, IN_SMEM] + [IN_VMEM] * (3 + len(batch)) + [ANYWHERE] * (len(arrays) - len(batch)),
        out_specs=IN_VMEM,
        scratch_shapes=scratch if last else [],
        input_output_aliases={} if last else {4: 0},
        compiler_params=pltpu.CompilerParams(vmem_limit_bytes=VMEM_BYTES),
        cost_estimate=pl.CostEstimate(
            flops=8 * rows * QH * keys * HD, bytes_accessed=4 * rows * QH * HD, transcendentals=rows * QH * keys
        ),
        name="attend_last" if last else "attend_more",
    )(page_table, hit_tokens, queries, shift, mass, *arrays)


def owner_kernel(devices, orders, kinds, hops, offset_ref, *refs):
    key_refs = refs[: len(kinds)]
    own_ref, other_ref = refs[len(kinds) :]
    me = lax.axis_index("seq")
    group_size = devices // REQS
    request = me // group_size
    rows = key_refs[0].shape[0]
    each = rows // devices
    kept = own_ref.shape[1]
    lane = lax.broadcasted_iota(jnp.int32, (1, rows), 1)
    row = lax.broadcasted_iota(jnp.int32, (2 * kept, rows), 0)
    wanted_row = jnp.where(row >= kept, row - kept, row)
    residue, landing = lane % devices, lane // devices
    bases = []
    for kind in kinds:
        source = me if kind[0] == "own" else source_of(me, kind[1], kind[2], orders)
        place = source % group_size
        if hops[0] is not None:
            place = source % 2
            for n, hop in enumerate(hops):
                place = place + jnp.where((source ^ me) // 2 == hop // 2, 2 * n, 0)
        bases.append(place * each)
    for g in range(KVH):
        turn = (me - offset_ref[request, g] + devices) % devices
        mine = jnp.where(residue == turn, landing, -kept - rows)
        others = jnp.where(residue == turn ^ (devices // REQS), landing, -kept - rows)
        wanted = jnp.where(row >= kept, others, mine)
        total = jnp.zeros((2 * kept, 2 * HD), jnp.float32)
        for ref, base in zip(key_refs, bases):
            chosen = wanted_row == wanted + base
            total = total + jnp.dot(
                jnp.where(chosen, 1.0, 0.0).astype(jnp.bfloat16),
                ref[:, g * 2 * HD : (g + 1) * 2 * HD],
                preferred_element_type=jnp.float32,
            )
        own_ref[g] = total[:kept].astype(own_ref.dtype)
        other_ref[g] = total[kept:].astype(other_ref.dtype)


def pick_for_owners(devices, orders, owner_offset, batch, hops):
    rows, _ = batch[0][1].shape
    kept = len(batch) * rows // devices
    piece = jax.ShapeDtypeStruct((KVH, kept, 2 * HD), batch[0][1].dtype)
    return pl.pallas_call(
        functools.partial(owner_kernel, devices, orders, tuple(kind for kind, _ in batch), hops),
        out_shape=(piece, piece),
        in_specs=[IN_SMEM] + [IN_VMEM] * len(batch),
        out_specs=(IN_VMEM, IN_VMEM),
        compiler_params=pltpu.CompilerParams(vmem_limit_bytes=VMEM_BYTES),
        name="pick_for_owners",
    )(owner_offset, *[value for _, value in batch])


def place_kernel(devices, spans, size, *refs):
    me = lax.axis_index("seq")
    group_size = devices // REQS
    request = me // group_size
    chip = (me % group_size) // 2
    kept = size // REQS
    out_ref = refs[-1]
    for n, hops in enumerate(spans):
        for side, req in enumerate((request, 1 - request)):
            ref = refs[2 * n + side]
            height = ref.shape[1] // len(hops)
            for k, hop in enumerate(hops):
                start = req * kept
                if hop is not None:
                    start = start + (chip ^ (hop // 2)) * height
                rows = pl.ds(pl.multiple_of(start, height), height)
                out_ref[0, :, rows] = ref[:, k * height : (k + 1) * height]


def place(devices, pieces, spans, size):
    flat = [array for pair in pieces for array in pair]
    heads, _, width = flat[0].shape
    return pl.pallas_call(
        functools.partial(place_kernel, devices, tuple(spans), size),
        out_shape=jax.ShapeDtypeStruct((1, heads, size, width), flat[0].dtype),
        in_specs=[IN_VMEM] * len(flat),
        out_specs=IN_VMEM,
        name="place",
    )(*flat)


def shards(queries, suffix_kv, kv_store, page_table, hit_tokens, owner_offset):
    devices = lax.axis_size("seq")
    orders = hop_bits(devices)
    steps = len(orders[0])
    partner = devices // REQS
    rows = suffix_kv.shape[0]

    held = [((), suffix_kv)]
    first_hop = swap_by_core(suffix_kv, orders, 0)
    own_page, other_page = fetch_pages(page_table, kv_store, devices)
    mate = swap(suffix_kv, 1)
    page_set = [
        own_page,
        swap(other_page, partner),
        swap_by_core(own_page, orders, 0),
        swap_wide(other_page, orders, partner),
    ]
    mass, shift = attend_first(orders, queries, suffix_kv, mate)
    quad = jnp.concatenate(page_set, axis=0)
    pages = [((), quad)]
    held.append(((0,), after(first_hop, shift)))
    for step in range(1, steps):
        held = held + [(path + (step,), swap_by_core(value, orders, step)) for path, value in held]
        pages = pages + [(path + (step,), swap_by_core(value, orders, step)) for path, value in pages]

    own_kind, mate_kind = ("own",), ("block", True, ())
    arrivals = []
    for path, value in held[1:]:
        arrivals.append([(("block", False, path), value), (("block", True, path), swap(value, 1))])
    page_arrivals = []
    for path, value in pages:
        page_arrivals += [(("pages", False, path), value), (("pages", True, path), swap(value, 1))]
    home = [(own_kind, suffix_kv), (mate_kind, mate)]

    each = 2 * rows // devices
    if steps == 2 and each % 16 == 0:
        x, z = orders[0]
        batches = [(home + arrivals[0] + arrivals[1], (0, x, z)), (arrivals[2], (x ^ z,))]
    else:
        batches = [(home + sum(arrivals, []), (None,))]
    pieces, spans = [], []
    for batch, hops in batches:
        mine, theirs = pick_for_owners(devices, orders, owner_offset, batch, hops)
        pieces.append((mine, swap(theirs, partner)))
        spans.append(hops)

    more = functools.partial(attend_more, devices, orders, page_table, hit_tokens, queries, shift)
    for n in range(0, len(arrivals) - 1, 2):
        mass = more(mass, sum(arrivals[n : min(n + 2, len(arrivals) - 1)], []), None)
    attention_out = more(mass, arrivals[-1] + page_arrivals, home + sum(arrivals[:-1], []))
    return (attention_out, place(devices, pieces, spans, REQS * partner * rows // devices))


def solution(mesh):
    in_specs = (
        P(("groups", "seq"), None),
        P(("groups", "seq"), None),
        P(("groups", "seq"), None, None),
        P("groups", None),
        P("groups"),
        P("groups", None),
    )
    out_specs = (P(("groups", "seq"), None), P(("groups", "seq"), None, None, None))
    return jax.shard_map(shards, mesh=mesh, in_specs=in_specs, out_specs=out_specs, check_vma=False)
```

```python
import functools

import jax
import jax.numpy as jnp
from jax import lax
from jax.experimental import pallas as pl
from jax.experimental.pallas import tpu as pltpu
from jax.sharding import PartitionSpec as P

HD = 128
QH = 32
KVH = 4
REQS = 2
PAGE = 8
SLOTS = 32
GQ = QH // KVH

LOG2E = 1.4426950408889634
OUT_OF_REACH = -1e30
CHUNK = 512
VMEM_BYTES = 16 * 1024 * 1024
OPEN_VMEM_BYTES = 58 * 1024 * 1024
SMALL_VMEM_BYTES = 6 * 1024 * 1024
SAFE_MASS = 1e36
CONTRACT_LAST = (((1,), (1,)), ((), ()))

IN_VMEM = pl.BlockSpec(memory_space=pltpu.VMEM)
IN_SMEM = pl.BlockSpec(memory_space=pltpu.SMEM)
ANYWHERE = pl.BlockSpec(memory_space=pl.ANY)
IN_HBM = pl.BlockSpec(memory_space=pltpu.HBM)


def hop_bits(devices):
    bits = []
    bit = 2
    while bit < devices // REQS:
        bits.append(bit)
        bit *= 2
    return (tuple(bits), tuple(reversed(bits)))


def pick(core, pair):
    return jnp.where(core == 0, pair[0], pair[1])


def swap(value, bit):
    route = [(i, i ^ bit) for i in range(lax.axis_size("seq"))]
    return lax.ppermute(value, "seq", route)


def swap_by_core(value, orders, step):
    route = [(i, i ^ orders[i % 2][step]) for i in range(lax.axis_size("seq"))]
    return lax.ppermute(value, "seq", route)


def swap_wide(value, orders, bit):
    route = [(i, i ^ bit ^ orders[i % 2][0]) for i in range(lax.axis_size("seq"))]
    return lax.ppermute(value, "seq", route)


def after(value, *earlier):
    return lax.optimization_barrier((value,) + earlier)[0]


def source_of(me, swapped, path, orders):
    at = me ^ 1 if swapped else me
    core = at % 2
    for step in path:
        at = at ^ pick(core, (orders[0][step], orders[1][step]))
    return at


def page_bias(me, devices, orders, places, table_ref, hit_ref):
    shape = (4 * PAGE, HD)
    token = lax.broadcasted_iota(jnp.int32, shape, 0)
    slot = token >> (PAGE.bit_length() - 1)
    stores = []
    for swapped, path in places:
        base = source_of(me, swapped, path, orders)
        hop = pick(base & 1, (orders[0][0], orders[1][0]))
        at = jnp.where(slot >= 2, base ^ hop, base)
        stores.append(jnp.where((slot & 1) == 1, at ^ (devices // REQS), at))
    store = jnp.concatenate(stores, axis=0)
    inside = jnp.concatenate([token & (PAGE - 1)] * len(places), axis=0)
    request = me // (devices // REQS)
    position = jnp.zeros_like(store)
    for j in range(table_ref.shape[1]):
        position = jnp.where(store == table_ref[request, j] >> (SLOTS.bit_length() - 1), j * PAGE, position)
    return bias_lanes(jnp.where(position + inside < hit_ref[request], 0.0, OUT_OF_REACH))


def open_kernel(devices, orders, places, table_hbm, hit_hbm, store_ref, *refs):
    own_ref, other_ref, bias_ref, table_ref, hit_ref, sems = refs
    table = pltpu.make_async_copy(table_hbm, table_ref, sems.at[2])
    hits = pltpu.make_async_copy(hit_hbm, hit_ref, sems.at[3])
    table.start()
    hits.start()
    me = lax.axis_index("seq")
    request = me // (devices // REQS)
    copies = []
    table.wait()
    for n, (req, page_ref) in enumerate(((1 - request, other_ref), (request, own_ref))):
        slot = jnp.int32(0)
        for j in range(table_ref.shape[1]):
            away = table_ref[req, j] - me * SLOTS
            slot = jnp.where((away >= 0) & (away < SLOTS), away, slot)
        copies.append(pltpu.make_async_copy(store_ref.at[slot], page_ref, sems.at[n]))
        copies[-1].start()
    hits.wait()
    bias_ref[...] = page_bias(me, devices, orders, places, table_ref, hit_ref)
    for copy in copies:
        copy.wait()


def open_up(devices, orders, places, page_table, hit_tokens, kv_store):
    page = jax.ShapeDtypeStruct(kv_store.shape[1:], kv_store.dtype)
    return pl.pallas_call(
        functools.partial(open_kernel, devices, orders, places),
        out_shape=(
            page,
            page,
            jax.ShapeDtypeStruct((4 * PAGE * len(places), HD), jnp.bfloat16),
        ),
        in_specs=[IN_HBM] * 3,
        out_specs=(IN_VMEM,) * 3,
        scratch_shapes=[
            pltpu.SMEM(page_table.shape, jnp.int32),
            pltpu.SMEM(hit_tokens.shape, jnp.int32),
            pltpu.SemaphoreType.DMA((4,)),
        ],
        compiler_params=pltpu.CompilerParams(vmem_limit_bytes=OPEN_VMEM_BYTES),
        name="open_up",
    )(page_table, hit_tokens, kv_store)


def pack_kernel(block_ref, *refs):
    page_refs, out_ref = refs[:-1], refs[-1]
    rows = block_ref.shape[0]
    out_ref[:rows] = block_ref[...]
    out_ref[rows:] = jnp.concatenate([ref[...] for ref in page_refs], axis=0)


def pack(block, pages):
    rows = block.shape[0] + sum(page.shape[0] for page in pages)
    return pl.pallas_call(
        pack_kernel,
        out_shape=jax.ShapeDtypeStruct((rows, block.shape[1]), block.dtype),
        in_specs=[IN_VMEM] * (1 + len(pages)),
        out_specs=IN_VMEM,
        compiler_params=pltpu.CompilerParams(vmem_limit_bytes=SMALL_VMEM_BYTES),
        name="pack",
    )(block, *pages)


def stack(refs, at):
    return jnp.concatenate([ref[first : first + count, at : at + HD] for ref, first, count in refs], axis=0)


def head_rows(q_ref, g):
    heads = range(g * GQ, (g + 1) * GQ)
    return jnp.concatenate([q_ref[:, h * HD : (h + 1) * HD] for h in heads], axis=0)


def with_ones(values):
    return jnp.concatenate([values, jnp.ones_like(values)], axis=1)


def shift_lanes(shift):
    lane = lax.broadcasted_iota(jnp.int32, shift.shape, 1)
    return jnp.where(lane == 0, -shift, jnp.where(lane == 1, 1.0, 0.0)).astype(jnp.bfloat16)


def bias_lanes(bias):
    lane = lax.broadcasted_iota(jnp.int32, bias.shape, 1)
    return jnp.where(lane == 0, 1.0, jnp.where(lane == 1, bias, 0.0)).astype(jnp.bfloat16)


def causal_bias(rows):
    t = lax.broadcasted_iota(jnp.int32, (rows, rows), 0)
    k = lax.broadcasted_iota(jnp.int32, (rows, rows), 1)
    return jnp.where(k <= t, 0.0, OUT_OF_REACH)


SCALE = HD**-0.5 * LOG2E


def first_kernel(orders, q_ref, own_ref, mate_ref, mass_ref, shift_ref):
    me = lax.axis_index("seq")
    rows = q_ref.shape[0]
    mate_bias = jnp.where(me % 2 == 1, 0.0, OUT_OF_REACH)
    bias = jnp.concatenate([causal_bias(rows), jnp.full((rows, rows), mate_bias, jnp.float32)], axis=1)
    refs = ((own_ref, 0, rows), (mate_ref, 0, rows))
    for g in range(KVH):
        at = g * 2 * HD
        scores = lax.dot_general(head_rows(q_ref, g), stack(refs, at), CONTRACT_LAST, preferred_element_type=jnp.float32)
        scores = (scores.reshape(GQ, rows, -1) + bias[None]).reshape(GQ * rows, -1)
        peak = jnp.max(scores, axis=1, keepdims=True)
        shift = jnp.broadcast_to(peak, (GQ * rows, HD)).astype(jnp.bfloat16).astype(jnp.float32)
        weights = jnp.exp2((scores - jnp.concatenate([shift, shift], axis=1)) * SCALE).astype(jnp.bfloat16)
        span = pl.ds(g * GQ * rows, GQ * rows)
        mass_ref[span, :] = jnp.dot(weights, with_ones(stack(refs, at + HD)), preferred_element_type=jnp.float32)
        shift_ref[span, :] = shift_lanes(shift)


def attend_first(orders, queries, own, mate):
    rows = queries.shape[0]
    return pl.pallas_call(
        functools.partial(first_kernel, orders),
        out_shape=(
            jax.ShapeDtypeStruct((QH * rows, 2 * HD), jnp.float32),
            jax.ShapeDtypeStruct((QH * rows, HD), jnp.bfloat16),
        ),
        in_specs=[IN_VMEM] * 3,
        out_specs=(IN_VMEM, IN_VMEM),
        compiler_params=pltpu.CompilerParams(vmem_limit_bytes=VMEM_BYTES),
        cost_estimate=pl.CostEstimate(
            flops=16 * rows * QH * rows * HD, bytes_accessed=4 * rows * QH * HD, transcendentals=2 * rows * QH * rows
        ),
        name="attend_first",
    )(queries, own, mate)


def block_bias(me, orders, kind, rows):
    if kind[0] == "own":
        return bias_lanes(jnp.zeros((rows, HD), jnp.float32))
    source = source_of(me, kind[1], kind[2], orders)
    return bias_lanes(jnp.full((rows, HD), jnp.where(source < me, 0.0, OUT_OF_REACH), jnp.float32))


def add_up(q_wide, group, bias, at):
    keys = jnp.concatenate([stack(group, at), bias], axis=1)
    scores = lax.dot_general(q_wide, keys, CONTRACT_LAST, preferred_element_type=jnp.float32)
    weights = jnp.exp2(scores * SCALE).astype(jnp.bfloat16)
    return jnp.dot(weights, with_ones(stack(group, at + HD)), preferred_element_type=jnp.float32)


def more_kernel(orders, kinds, q_ref, shift_ref, mass_ref, *refs):
    out_ref = refs[-1]
    me = lax.axis_index("seq")
    rows = q_ref.shape[0]
    group = [(ref, 0, rows) for ref in refs[:-1]]
    bias = jnp.concatenate([block_bias(me, orders, kind, rows) for kind in kinds], axis=0)
    for g in range(KVH):
        span = pl.ds(g * GQ * rows, GQ * rows)
        q_wide = jnp.concatenate([head_rows(q_ref, g), shift_ref[span, :]], axis=1)
        out_ref[span, :] = mass_ref[span, :] + add_up(q_wide, group, bias, g * 2 * HD)


def attend_more(orders, queries, shift, mass, batch):
    rows = queries.shape[0]
    keys = rows * len(batch)
    return pl.pallas_call(
        functools.partial(more_kernel, orders, tuple(kind for kind, _ in batch)),
        out_shape=jax.ShapeDtypeStruct(mass.shape, mass.dtype),
        in_specs=[IN_VMEM] * (3 + len(batch)),
        out_specs=IN_VMEM,
        input_output_aliases={2: 0},
        compiler_params=pltpu.CompilerParams(vmem_limit_bytes=VMEM_BYTES),
        cost_estimate=pl.CostEstimate(
            flops=8 * rows * QH * keys * HD, bytes_accessed=4 * rows * QH * HD, transcendentals=rows * QH * keys
        ),
        name="attend_more",
    )(queries, shift, mass, *[value for _, value in batch])


def last_kernel(orders, kinds, page_count, other_kinds, q_ref, shift_ref, mass_ref, bias_ref, *refs):
    me = lax.axis_index("seq")
    rows = q_ref.shape[0]
    block_refs = refs[: len(kinds)]
    page_refs = refs[len(kinds) : len(kinds) + page_count]
    other_refs = refs[len(kinds) + page_count : -9]
    out_ref, kept_ref, wrong_ref, top_ref, denominator_ref, total_ref, block_ref, sems, sem = refs[-9:]
    held = 4 * PAGE
    group = [(ref, 0, rows) for ref in block_refs] + [(ref, rows, held) for ref in page_refs]
    biases = [block_bias(me, orders, kind, rows) for kind in kinds] + [bias_ref[...]]
    bias = jnp.concatenate(biases, axis=0)
    wrong_ref[...] = jnp.zeros_like(wrong_ref)
    width = GQ * HD

    def write(g):
        return pltpu.make_async_copy(kept_ref.at[g], out_ref.at[:, pl.ds(g * width, width)], sems.at[g])

    for g in range(KVH):
        span = pl.ds(g * GQ * rows, GQ * rows)
        q_wide = jnp.concatenate([head_rows(q_ref, g), shift_ref[span, :]], axis=1)
        mass = mass_ref[span, :] + add_up(q_wide, group, bias, g * 2 * HD)
        total, denominator = mass[:, :HD], mass[:, HD:]
        wrong = jnp.where(denominator < SAFE_MASS, 0.0, 1.0)
        wrong_ref[...] = jnp.maximum(wrong_ref[...], jnp.max(wrong.reshape(-1, 8, HD), axis=0))
        attended = (total / denominator).astype(kept_ref.dtype)
        for n in range(GQ):
            kept_ref[g, :, n * HD : (n + 1) * HD] = attended[n * rows : (n + 1) * rows]
        write(g).start()
    for g in range(KVH):
        write(g).wait()

    @pl.when(jnp.max(wrong_ref[...]) > 0.0)
    def _():
        top_ref[...] = jnp.full_like(top_ref, OUT_OF_REACH)
        denominator_ref[...] = jnp.zeros_like(denominator_ref)
        total_ref[...] = jnp.zeros_like(total_ref)
        no_shift = shift_lanes(jnp.zeros((rows, HD), jnp.float32))

        def take(ref, first, count, lanes, causal):
            def one_head(n, carried):
                g, h = n // GQ, n % GQ
                at = pl.multiple_of(g * 2 * HD, 2 * HD)
                span = pl.ds(pl.multiple_of(n * rows, rows), rows)
                q = q_ref[:, pl.ds(pl.multiple_of(n * HD, HD), HD)]
                keys = jnp.concatenate([ref[first : first + count, pl.ds(at, HD)], lanes], axis=1)
                scores = lax.dot_general(
                    jnp.concatenate([q, no_shift], axis=1), keys, CONTRACT_LAST, preferred_element_type=jnp.float32
                )
                if causal:
                    scores = scores + causal_bias(rows)
                top = top_ref[span, :]
                new_top = jnp.maximum(top, jnp.max(scores, axis=1, keepdims=True))
                weights = jnp.exp2((scores - new_top[:, :count]) * SCALE)
                factor = jnp.exp2((top - new_top) * SCALE)
                top_ref[span, :] = new_top
                denominator_ref[span, :] = denominator_ref[span, :] * factor + jnp.sum(weights, axis=1, keepdims=True)
                total_ref[span, :] = total_ref[span, :] * factor + jnp.dot(
                    weights.astype(jnp.bfloat16),
                    ref[first : first + count, pl.ds(at + HD, HD)],
                    preferred_element_type=jnp.float32,
                )
                return carried

            lax.fori_loop(0, QH, one_head, 0)

        for kind, ref in zip(other_kinds, other_refs):
            copy = pltpu.make_async_copy(ref.at[pl.ds(0, rows)], block_ref, sem)
            copy.start()
            copy.wait()
            take(block_ref, 0, rows, block_bias(me, orders, kind, rows), kind[0] == "own")
        for kind, ref in zip(kinds, block_refs):
            take(ref, 0, rows, block_bias(me, orders, kind, rows), False)
        for n, ref in enumerate(page_refs):
            take(ref, rows, held, bias_ref[n * held : (n + 1) * held], False)
        for g in range(KVH):
            for n in range(GQ):
                span = pl.ds((g * GQ + n) * rows, rows)
                attended = total_ref[span, :] / denominator_ref[span, :]
                kept_ref[g, :, n * HD : (n + 1) * HD] = attended.astype(kept_ref.dtype)
            write(g).start()
        for g in range(KVH):
            write(g).wait()


def attend_last(orders, queries, shift, mass, bias, batch, pages, others):
    rows = queries.shape[0]
    keys = rows * len(batch) + bias.shape[0]
    width = 2 * KVH * HD
    return pl.pallas_call(
        functools.partial(
            last_kernel, orders, tuple(kind for kind, _ in batch), len(pages), tuple(kind for kind, _ in others)
        ),
        out_shape=jax.ShapeDtypeStruct((rows, QH * HD), queries.dtype),
        in_specs=[IN_VMEM] * (4 + len(batch) + len(pages)) + [ANYWHERE] * len(others),
        out_specs=ANYWHERE,
        scratch_shapes=[
            pltpu.VMEM((KVH, rows, GQ * HD), queries.dtype),
            pltpu.VMEM((8, HD), jnp.float32),
            *[pltpu.VMEM((QH * rows, HD), jnp.float32)] * 3,
            pltpu.VMEM((rows, width), jnp.bfloat16),
            pltpu.SemaphoreType.DMA((KVH,)),
            pltpu.SemaphoreType.DMA,
        ],
        compiler_params=pltpu.CompilerParams(vmem_limit_bytes=VMEM_BYTES),
        cost_estimate=pl.CostEstimate(
            flops=8 * rows * QH * keys * HD, bytes_accessed=4 * rows * QH * HD, transcendentals=rows * QH * keys
        ),
        name="attend_last",
    )(queries, shift, mass, bias, *[value for _, value in batch], *pages, *[value for _, value in others])


def owner_kernel(devices, orders, rows, kinds, hops, offset_ref, *refs):
    key_refs = refs[: len(kinds)]
    own_ref, other_ref = refs[len(kinds) :]
    me = lax.axis_index("seq")
    group_size = devices // REQS
    request = me // group_size
    each = rows // devices
    kept = own_ref.shape[1]
    lane = lax.broadcasted_iota(jnp.int32, (1, rows), 1)
    row = lax.broadcasted_iota(jnp.int32, (2 * kept, rows), 0)
    wanted_row = jnp.where(row >= kept, row - kept, row)
    residue, landing = lane % devices, lane // devices
    bases = []
    for kind in kinds:
        source = me if kind[0] == "own" else source_of(me, kind[1], kind[2], orders)
        place = source % group_size
        if hops[0] is not None:
            place = source % 2
            for n, hop in enumerate(hops):
                place = place + jnp.where((source ^ me) // 2 == hop // 2, 2 * n, 0)
        bases.append(place * each)
    for g in range(KVH):
        turn = (me - offset_ref[request, g] + devices) % devices
        mine = jnp.where(residue == turn, landing, -kept - rows)
        others = jnp.where(residue == turn ^ (devices // REQS), landing, -kept - rows)
        wanted = jnp.where(row >= kept, others, mine)
        total = jnp.zeros((2 * kept, 2 * HD), jnp.float32)
        for ref, base in zip(key_refs, bases):
            chosen = wanted_row == wanted + base
            total = total + jnp.dot(
                jnp.where(chosen, 1.0, 0.0).astype(jnp.bfloat16),
                ref[:rows, g * 2 * HD : (g + 1) * 2 * HD],
                preferred_element_type=jnp.float32,
            )
        own_ref[g] = total[:kept].astype(own_ref.dtype)
        other_ref[g] = total[kept:].astype(other_ref.dtype)


def pick_for_owners(devices, orders, owner_offset, rows, batch, hops):
    kept = len(batch) * rows // devices
    piece = jax.ShapeDtypeStruct((KVH, kept, 2 * HD), batch[0][1].dtype)
    return pl.pallas_call(
        functools.partial(owner_kernel, devices, orders, rows, tuple(kind for kind, _ in batch), hops),
        out_shape=(piece, piece),
        in_specs=[IN_SMEM] + [IN_VMEM] * len(batch),
        out_specs=(IN_VMEM, IN_VMEM),
        compiler_params=pltpu.CompilerParams(vmem_limit_bytes=SMALL_VMEM_BYTES),
        name="pick_for_owners",
    )(owner_offset, *[value for _, value in batch])


def place_kernel(devices, spans, size, *refs):
    me = lax.axis_index("seq")
    group_size = devices // REQS
    request = me // group_size
    chip = (me % group_size) // 2
    kept = size // REQS
    out_ref = refs[-1]
    for n, hops in enumerate(spans):
        for side, req in enumerate((request, 1 - request)):
            ref = refs[2 * n + side]
            height = ref.shape[1] // len(hops)
            for k, hop in enumerate(hops):
                start = req * kept
                if hop is not None:
                    start = start + (chip ^ (hop // 2)) * height
                rows = pl.ds(pl.multiple_of(start, height), height)
                out_ref[0, :, rows] = ref[:, k * height : (k + 1) * height]


def place(devices, pieces, spans, size):
    flat = [array for pair in pieces for array in pair]
    heads, _, width = flat[0].shape
    return pl.pallas_call(
        functools.partial(place_kernel, devices, tuple(spans), size),
        out_shape=jax.ShapeDtypeStruct((1, heads, size, width), flat[0].dtype),
        in_specs=[IN_VMEM] * len(flat),
        out_specs=IN_VMEM,
        compiler_params=pltpu.CompilerParams(vmem_limit_bytes=SMALL_VMEM_BYTES),
        name="place",
    )(*flat)


def shards(queries, suffix_kv, kv_store, page_table, hit_tokens, owner_offset):
    devices = lax.axis_size("seq")
    orders = hop_bits(devices)
    steps = len(orders[0])
    partner = devices // REQS
    rows = suffix_kv.shape[0]

    page_paths = [()]
    for step in range(1, steps):
        page_paths = page_paths + [path + (step,) for path in page_paths]
    places = tuple((swapped, path) for path in page_paths for swapped in (False, True))

    first_hop = swap_by_core(suffix_kv, orders, 0)
    mate = swap(suffix_kv, 1)
    own_page, other_page, bias = open_up(devices, orders, places, page_table, hit_tokens, kv_store)
    page_set = [
        own_page,
        swap(other_page, partner),
        swap_by_core(own_page, orders, 0),
        swap_wide(after(other_page, mate), orders, partner),
    ]
    mass, shift = attend_first(orders, queries, suffix_kv, mate)
    held = [((), suffix_kv), ((0,), pack(first_hop, page_set))]
    for step in range(1, steps):
        held = held + [(path + (step,), swap_by_core(value, orders, step)) for path, value in held]

    arrivals, pages = [], {}

    def exchange(moved, *earlier):
        for path, value in moved:
            swapped_value = swap(after(value, *earlier) if earlier else value, 1)
            arrivals.append([(("block", False, path), value), (("block", True, path), swapped_value)])
            if path[0] == 0:
                pages[(False, path[1:])], pages[(True, path[1:])] = value, swapped_value

    def to_owners(batch, hops):
        mine, theirs = pick_for_owners(devices, orders, owner_offset, rows, batch, hops)
        spans.append(hops)
        pieces.append((mine, swap(theirs, partner)))
        return theirs

    home = [(("own",), suffix_kv), (("block", True, ()), after(mate, shift))]
    pieces, spans = [], []
    if steps == 2 and (2 * rows // devices) % 16 == 0:
        near, across = orders[0], orders[0][0] ^ orders[0][1]
        exchange(held[1:3])
        sent = to_owners(home + arrivals[0] + arrivals[1], (0,) + near)
        exchange(held[3:], sent)
        to_owners(arrivals[2], (across,))
    else:
        exchange(held[1:])
        to_owners(home + sum(arrivals, []), (None,))

    for n in range(0, len(arrivals) - 1, 2):
        mass = attend_more(orders, queries, shift, mass, sum(arrivals[n : min(n + 2, len(arrivals) - 1)], []))
    attention_out = attend_last(
        orders,
        queries,
        shift,
        mass,
        bias,
        arrivals[-1],
        [pages[place] for place in places],
        home + sum(arrivals[:-1], []),
    )
    return (attention_out, place(devices, pieces, spans, REQS * partner * rows // devices))


def solution(mesh):
    in_specs = (
        P(("groups", "seq"), None),
        P(("groups", "seq"), None),
        P(("groups", "seq"), None, None),
        P("groups", None),
        P("groups"),
        P("groups", None),
    )
    out_specs = (P(("groups", "seq"), None), P(("groups", "seq"), None, None, None))
    return jax.shard_map(shards, mesh=mesh, in_specs=in_specs, out_specs=out_specs, check_vma=False)
```

```python
import functools

import jax
import jax.numpy as jnp
from jax import lax
from jax.experimental import pallas as pl
from jax.experimental.pallas import tpu as pltpu
from jax.sharding import PartitionSpec as P

HD = 128
QH = 32
KVH = 4
REQS = 2
PAGE = 8
SLOTS = 32
GQ = QH // KVH

LOG2E = 1.4426950408889634
OUT_OF_REACH = -1e30
CHUNK = 512
VMEM_BYTES = 16 * 1024 * 1024
OPEN_VMEM_BYTES = 58 * 1024 * 1024
SMALL_VMEM_BYTES = 6 * 1024 * 1024
SAFE_MASS = 1e36
CONTRACT_LAST = (((1,), (1,)), ((), ()))

IN_VMEM = pl.BlockSpec(memory_space=pltpu.VMEM)
IN_SMEM = pl.BlockSpec(memory_space=pltpu.SMEM)
ANYWHERE = pl.BlockSpec(memory_space=pl.ANY)
IN_HBM = pl.BlockSpec(memory_space=pltpu.HBM)


def hop_bits(devices):
    bits = []
    bit = 2
    while bit < devices // REQS:
        bits.append(bit)
        bit *= 2
    return (tuple(bits), tuple(reversed(bits)))


def pick(core, pair):
    return jnp.where(core == 0, pair[0], pair[1])


def swap(value, bit):
    route = [(i, i ^ bit) for i in range(lax.axis_size("seq"))]
    return lax.ppermute(value, "seq", route)


def swap_by_core(value, orders, step):
    route = [(i, i ^ orders[i % 2][step]) for i in range(lax.axis_size("seq"))]
    return lax.ppermute(value, "seq", route)


def after(value, *earlier):
    return lax.optimization_barrier((value,) + earlier)[0]


def source_of(me, swapped, path, orders):
    at = me ^ 1 if swapped else me
    core = at % 2
    for step in path:
        at = at ^ pick(core, (orders[0][step], orders[1][step]))
    return at


def page_bias(me, devices, orders, places, table_ref, hit_ref):
    shape = (4 * PAGE, HD)
    token = lax.broadcasted_iota(jnp.int32, shape, 0)
    slot = token >> (PAGE.bit_length() - 1)
    stores = []
    for swapped, path in places:
        base = source_of(me, swapped, path, orders)
        hop = pick(base & 1, (orders[0][0], orders[1][0]))
        at = jnp.where(slot >= 2, base ^ hop, base)
        stores.append(jnp.where((slot & 1) == 1, at ^ (devices // REQS), at))
    store = jnp.concatenate(stores, axis=0)
    inside = jnp.concatenate([token & (PAGE - 1)] * len(places), axis=0)
    request = me // (devices // REQS)
    position = jnp.zeros_like(store)
    for j in range(table_ref.shape[1]):
        position = jnp.where(store == table_ref[request, j] >> (SLOTS.bit_length() - 1), j * PAGE, position)
    return bias_lanes(jnp.where(position + inside < hit_ref[request], 0.0, OUT_OF_REACH))


def open_kernel(devices, orders, places, table_hbm, hit_hbm, store_ref, *refs):
    own_ref, other_ref, bias_ref, table_ref, hit_ref, sems = refs
    table = pltpu.make_async_copy(table_hbm, table_ref, sems.at[2])
    hits = pltpu.make_async_copy(hit_hbm, hit_ref, sems.at[3])
    table.start()
    hits.start()
    me = lax.axis_index("seq")
    request = me // (devices // REQS)
    copies = []
    table.wait()
    for n, (req, page_ref) in enumerate(((1 - request, other_ref), (request, own_ref))):
        slot = jnp.int32(0)
        for j in range(table_ref.shape[1]):
            away = table_ref[req, j] - me * SLOTS
            slot = jnp.where((away >= 0) & (away < SLOTS), away, slot)
        copies.append(pltpu.make_async_copy(store_ref.at[slot], page_ref, sems.at[n]))
        copies[-1].start()
    hits.wait()
    bias_ref[...] = page_bias(me, devices, orders, places, table_ref, hit_ref)
    for copy in copies:
        copy.wait()


def open_up(devices, orders, places, page_table, hit_tokens, kv_store):
    page = jax.ShapeDtypeStruct(kv_store.shape[1:], kv_store.dtype)
    return pl.pallas_call(
        functools.partial(open_kernel, devices, orders, places),
        out_shape=(
            page,
            page,
            jax.ShapeDtypeStruct((4 * PAGE * len(places), HD), jnp.bfloat16),
        ),
        in_specs=[IN_HBM] * 3,
        out_specs=(IN_VMEM,) * 3,
        scratch_shapes=[
            pltpu.SMEM(page_table.shape, jnp.int32),
            pltpu.SMEM(hit_tokens.shape, jnp.int32),
            pltpu.SemaphoreType.DMA((4,)),
        ],
        compiler_params=pltpu.CompilerParams(vmem_limit_bytes=OPEN_VMEM_BYTES),
        name="open_up",
    )(page_table, hit_tokens, kv_store)


def pack_kernel(*refs):
    refs[-1][...] = jnp.concatenate([ref[...] for ref in refs[:-1]], axis=0)


def pack(pages):
    rows = sum(page.shape[0] for page in pages)
    return pl.pallas_call(
        pack_kernel,
        out_shape=jax.ShapeDtypeStruct((rows, pages[0].shape[1]), pages[0].dtype),
        in_specs=[IN_VMEM] * len(pages),
        out_specs=IN_VMEM,
        compiler_params=pltpu.CompilerParams(vmem_limit_bytes=SMALL_VMEM_BYTES),
        name="pack",
    )(*pages)


def stack(refs, at):
    return jnp.concatenate([ref[first : first + count, at : at + HD] for ref, first, count in refs], axis=0)


def head_rows(q_ref, g):
    heads = range(g * GQ, (g + 1) * GQ)
    return jnp.concatenate([q_ref[:, h * HD : (h + 1) * HD] for h in heads], axis=0)


def with_ones(values):
    return jnp.concatenate([values, jnp.ones_like(values)], axis=1)


def shift_lanes(shift):
    lane = lax.broadcasted_iota(jnp.int32, shift.shape, 1)
    return jnp.where(lane == 0, -shift, jnp.where(lane == 1, 1.0, 0.0)).astype(jnp.bfloat16)


def bias_lanes(bias):
    lane = lax.broadcasted_iota(jnp.int32, bias.shape, 1)
    return jnp.where(lane == 0, 1.0, jnp.where(lane == 1, bias, 0.0)).astype(jnp.bfloat16)


def causal_bias(rows):
    t = lax.broadcasted_iota(jnp.int32, (rows, rows), 0)
    k = lax.broadcasted_iota(jnp.int32, (rows, rows), 1)
    return jnp.where(k <= t, 0.0, OUT_OF_REACH)


SCALE = HD**-0.5 * LOG2E


def first_kernel(orders, q_ref, own_ref, mate_ref, mass_ref, shift_ref):
    me = lax.axis_index("seq")
    rows = q_ref.shape[0]
    mate_bias = jnp.where(me % 2 == 1, 0.0, OUT_OF_REACH)
    bias = jnp.concatenate([causal_bias(rows), jnp.full((rows, rows), mate_bias, jnp.float32)], axis=1)
    refs = ((own_ref, 0, rows), (mate_ref, 0, rows))
    for g in range(KVH):
        at = g * 2 * HD
        scores = lax.dot_general(head_rows(q_ref, g), stack(refs, at), CONTRACT_LAST, preferred_element_type=jnp.float32)
        scores = (scores.reshape(GQ, rows, -1) + bias[None]).reshape(GQ * rows, -1)
        peak = jnp.max(scores, axis=1, keepdims=True)
        shift = jnp.broadcast_to(peak, (GQ * rows, HD)).astype(jnp.bfloat16).astype(jnp.float32)
        weights = jnp.exp2((scores - jnp.concatenate([shift, shift], axis=1)) * SCALE).astype(jnp.bfloat16)
        span = pl.ds(g * GQ * rows, GQ * rows)
        mass_ref[span, :] = jnp.dot(weights, with_ones(stack(refs, at + HD)), preferred_element_type=jnp.float32)
        shift_ref[span, :] = shift_lanes(shift)


def attend_first(orders, queries, own, mate):
    rows = queries.shape[0]
    return pl.pallas_call(
        functools.partial(first_kernel, orders),
        out_shape=(
            jax.ShapeDtypeStruct((QH * rows, 2 * HD), jnp.float32),
            jax.ShapeDtypeStruct((QH * rows, HD), jnp.bfloat16),
        ),
        in_specs=[IN_VMEM] * 3,
        out_specs=(IN_VMEM, IN_VMEM),
        compiler_params=pltpu.CompilerParams(vmem_limit_bytes=VMEM_BYTES),
        cost_estimate=pl.CostEstimate(
            flops=16 * rows * QH * rows * HD, bytes_accessed=4 * rows * QH * HD, transcendentals=2 * rows * QH * rows
        ),
        name="attend_first",
    )(queries, own, mate)


def block_bias(me, orders, kind, rows):
    if kind[0] == "own":
        return bias_lanes(jnp.zeros((rows, HD), jnp.float32))
    source = source_of(me, kind[1], kind[2], orders)
    return bias_lanes(jnp.full((rows, HD), jnp.where(source < me, 0.0, OUT_OF_REACH), jnp.float32))


def add_up(q_wide, group, bias, at):
    keys = jnp.concatenate([stack(group, at), bias], axis=1)
    scores = lax.dot_general(q_wide, keys, CONTRACT_LAST, preferred_element_type=jnp.float32)
    weights = jnp.exp2(scores * SCALE).astype(jnp.bfloat16)
    return jnp.dot(weights, with_ones(stack(group, at + HD)), preferred_element_type=jnp.float32)


def more_kernel(orders, kinds, q_ref, shift_ref, mass_ref, *refs):
    out_ref = refs[-1]
    me = lax.axis_index("seq")
    rows = q_ref.shape[0]
    group = [(ref, 0, rows) for ref in refs[:-1]]
    bias = jnp.concatenate([block_bias(me, orders, kind, rows) for kind in kinds], axis=0)
    for g in range(KVH):
        span = pl.ds(g * GQ * rows, GQ * rows)
        q_wide = jnp.concatenate([head_rows(q_ref, g), shift_ref[span, :]], axis=1)
        out_ref[span, :] = mass_ref[span, :] + add_up(q_wide, group, bias, g * 2 * HD)


def attend_more(orders, queries, shift, mass, batch):
    rows = queries.shape[0]
    keys = rows * len(batch)
    return pl.pallas_call(
        functools.partial(more_kernel, orders, tuple(kind for kind, _ in batch)),
        out_shape=jax.ShapeDtypeStruct(mass.shape, mass.dtype),
        in_specs=[IN_VMEM] * (3 + len(batch)),
        out_specs=IN_VMEM,
        input_output_aliases={2: 0},
        compiler_params=pltpu.CompilerParams(vmem_limit_bytes=VMEM_BYTES),
        cost_estimate=pl.CostEstimate(
            flops=8 * rows * QH * keys * HD, bytes_accessed=4 * rows * QH * HD, transcendentals=rows * QH * keys
        ),
        name="attend_more",
    )(queries, shift, mass, *[value for _, value in batch])


def last_kernel(orders, kinds, page_count, other_kinds, q_ref, shift_ref, mass_ref, bias_ref, *refs):
    me = lax.axis_index("seq")
    rows = q_ref.shape[0]
    block_refs = refs[: len(kinds)]
    page_refs = refs[len(kinds) : len(kinds) + page_count]
    other_refs = refs[len(kinds) + page_count : -9]
    out_ref, kept_ref, wrong_ref, top_ref, denominator_ref, total_ref, block_ref, sems, sem = refs[-9:]
    held = 4 * PAGE
    group = [(ref, 0, rows) for ref in block_refs] + [(ref, 0, held) for ref in page_refs]
    biases = [block_bias(me, orders, kind, rows) for kind in kinds] + [bias_ref[...]]
    bias = jnp.concatenate(biases, axis=0)
    wrong_ref[...] = jnp.zeros_like(wrong_ref)
    width = GQ * HD

    def write(g):
        return pltpu.make_async_copy(kept_ref.at[g], out_ref.at[:, pl.ds(g * width, width)], sems.at[g])

    for g in range(KVH):
        span = pl.ds(g * GQ * rows, GQ * rows)
        q_wide = jnp.concatenate([head_rows(q_ref, g), shift_ref[span, :]], axis=1)
        mass = mass_ref[span, :] + add_up(q_wide, group, bias, g * 2 * HD)
        total, denominator = mass[:, :HD], mass[:, HD:]
        wrong = jnp.where(denominator < SAFE_MASS, 0.0, 1.0)
        wrong_ref[...] = jnp.maximum(wrong_ref[...], jnp.max(wrong.reshape(-1, 8, HD), axis=0))
        attended = (total / denominator).astype(kept_ref.dtype)
        for n in range(GQ):
            kept_ref[g, :, n * HD : (n + 1) * HD] = attended[n * rows : (n + 1) * rows]
        write(g).start()
    for g in range(KVH):
        write(g).wait()

    @pl.when(jnp.max(wrong_ref[...]) > 0.0)
    def _():
        top_ref[...] = jnp.full_like(top_ref, OUT_OF_REACH)
        denominator_ref[...] = jnp.zeros_like(denominator_ref)
        total_ref[...] = jnp.zeros_like(total_ref)
        no_shift = shift_lanes(jnp.zeros((rows, HD), jnp.float32))

        def take(ref, first, count, lanes, causal):
            def one_head(n, carried):
                g, h = n // GQ, n % GQ
                at = pl.multiple_of(g * 2 * HD, 2 * HD)
                span = pl.ds(pl.multiple_of(n * rows, rows), rows)
                q = q_ref[:, pl.ds(pl.multiple_of(n * HD, HD), HD)]
                keys = jnp.concatenate([ref[first : first + count, pl.ds(at, HD)], lanes], axis=1)
                scores = lax.dot_general(
                    jnp.concatenate([q, no_shift], axis=1), keys, CONTRACT_LAST, preferred_element_type=jnp.float32
                )
                if causal:
                    scores = scores + causal_bias(rows)
                top = top_ref[span, :]
                new_top = jnp.maximum(top, jnp.max(scores, axis=1, keepdims=True))
                weights = jnp.exp2((scores - new_top[:, :count]) * SCALE)
                factor = jnp.exp2((top - new_top) * SCALE)
                top_ref[span, :] = new_top
                denominator_ref[span, :] = denominator_ref[span, :] * factor + jnp.sum(weights, axis=1, keepdims=True)
                total_ref[span, :] = total_ref[span, :] * factor + jnp.dot(
                    weights.astype(jnp.bfloat16),
                    ref[first : first + count, pl.ds(at + HD, HD)],
                    preferred_element_type=jnp.float32,
                )
                return carried

            lax.fori_loop(0, QH, one_head, 0)

        for kind, ref in zip(other_kinds, other_refs):
            copy = pltpu.make_async_copy(ref.at[pl.ds(0, rows)], block_ref, sem)
            copy.start()
            copy.wait()
            take(block_ref, 0, rows, block_bias(me, orders, kind, rows), kind[0] == "own")
        for kind, ref in zip(kinds, block_refs):
            take(ref, 0, rows, block_bias(me, orders, kind, rows), False)
        for n, ref in enumerate(page_refs):
            take(ref, 0, held, bias_ref[n * held : (n + 1) * held], False)
        for g in range(KVH):
            for n in range(GQ):
                span = pl.ds((g * GQ + n) * rows, rows)
                attended = total_ref[span, :] / denominator_ref[span, :]
                kept_ref[g, :, n * HD : (n + 1) * HD] = attended.astype(kept_ref.dtype)
            write(g).start()
        for g in range(KVH):
            write(g).wait()


def attend_last(orders, queries, shift, mass, bias, batch, pages, others):
    rows = queries.shape[0]
    keys = rows * len(batch) + bias.shape[0]
    width = 2 * KVH * HD
    return pl.pallas_call(
        functools.partial(
            last_kernel, orders, tuple(kind for kind, _ in batch), len(pages), tuple(kind for kind, _ in others)
        ),
        out_shape=jax.ShapeDtypeStruct((rows, QH * HD), queries.dtype),
        in_specs=[IN_VMEM] * (4 + len(batch) + len(pages)) + [ANYWHERE] * len(others),
        out_specs=ANYWHERE,
        scratch_shapes=[
            pltpu.VMEM((KVH, rows, GQ * HD), queries.dtype),
            pltpu.VMEM((8, HD), jnp.float32),
            *[pltpu.VMEM((QH * rows, HD), jnp.float32)] * 3,
            pltpu.VMEM((rows, width), jnp.bfloat16),
            pltpu.SemaphoreType.DMA((KVH,)),
            pltpu.SemaphoreType.DMA,
        ],
        compiler_params=pltpu.CompilerParams(vmem_limit_bytes=VMEM_BYTES),
        cost_estimate=pl.CostEstimate(
            flops=8 * rows * QH * keys * HD, bytes_accessed=4 * rows * QH * HD, transcendentals=rows * QH * keys
        ),
        name="attend_last",
    )(queries, shift, mass, bias, *[value for _, value in batch], *pages, *[value for _, value in others])


def owner_kernel(devices, orders, rows, kinds, hops, offset_ref, *refs):
    key_refs = refs[: len(kinds)]
    own_ref, other_ref = refs[len(kinds) :]
    me = lax.axis_index("seq")
    group_size = devices // REQS
    request = me // group_size
    each = rows // devices
    kept = own_ref.shape[1]
    lane = lax.broadcasted_iota(jnp.int32, (1, rows), 1)
    row = lax.broadcasted_iota(jnp.int32, (2 * kept, rows), 0)
    wanted_row = jnp.where(row >= kept, row - kept, row)
    residue, landing = lane % devices, lane // devices
    bases = []
    for kind in kinds:
        source = me if kind[0] == "own" else source_of(me, kind[1], kind[2], orders)
        place = source % group_size
        if hops[0] is not None:
            place = source % 2
            for n, hop in enumerate(hops):
                place = place + jnp.where((source ^ me) // 2 == hop // 2, 2 * n, 0)
        bases.append(place * each)
    for g in range(KVH):
        turn = (me - offset_ref[request, g] + devices) % devices
        mine = jnp.where(residue == turn, landing, -kept - rows)
        others = jnp.where(residue == turn ^ (devices // REQS), landing, -kept - rows)
        wanted = jnp.where(row >= kept, others, mine)
        total = jnp.zeros((2 * kept, 2 * HD), jnp.float32)
        for ref, base in zip(key_refs, bases):
            chosen = wanted_row == wanted + base
            total = total + jnp.dot(
                jnp.where(chosen, 1.0, 0.0).astype(jnp.bfloat16),
                ref[:rows, g * 2 * HD : (g + 1) * 2 * HD],
                preferred_element_type=jnp.float32,
            )
        own_ref[g] = total[:kept].astype(own_ref.dtype)
        other_ref[g] = total[kept:].astype(other_ref.dtype)


def pick_for_owners(devices, orders, owner_offset, rows, batch, hops):
    kept = len(batch) * rows // devices
    piece = jax.ShapeDtypeStruct((KVH, kept, 2 * HD), batch[0][1].dtype)
    return pl.pallas_call(
        functools.partial(owner_kernel, devices, orders, rows, tuple(kind for kind, _ in batch), hops),
        out_shape=(piece, piece),
        in_specs=[IN_SMEM] + [IN_VMEM] * len(batch),
        out_specs=(IN_VMEM, IN_VMEM),
        compiler_params=pltpu.CompilerParams(vmem_limit_bytes=SMALL_VMEM_BYTES),
        name="pick_for_owners",
    )(owner_offset, *[value for _, value in batch])


def place_kernel(devices, spans, size, *refs):
    me = lax.axis_index("seq")
    group_size = devices // REQS
    request = me // group_size
    chip = (me % group_size) // 2
    kept = size // REQS
    out_ref = refs[-1]
    for n, hops in enumerate(spans):
        for side, req in enumerate((request, 1 - request)):
            ref = refs[2 * n + side]
            height = ref.shape[1] // len(hops)
            for k, hop in enumerate(hops):
                start = req * kept
                if hop is not None:
                    start = start + (chip ^ (hop // 2)) * height
                rows = pl.ds(pl.multiple_of(start, height), height)
                out_ref[0, :, rows] = ref[:, k * height : (k + 1) * height]


def place(devices, pieces, spans, size):
    flat = [array for pair in pieces for array in pair]
    heads, _, width = flat[0].shape
    return pl.pallas_call(
        functools.partial(place_kernel, devices, tuple(spans), size),
        out_shape=jax.ShapeDtypeStruct((1, heads, size, width), flat[0].dtype),
        in_specs=[IN_VMEM] * len(flat),
        out_specs=IN_VMEM,
        compiler_params=pltpu.CompilerParams(vmem_limit_bytes=SMALL_VMEM_BYTES),
        name="place",
    )(*flat)


def shards(queries, suffix_kv, kv_store, page_table, hit_tokens, owner_offset):
    devices = lax.axis_size("seq")
    orders = hop_bits(devices)
    steps = len(orders[0])
    partner = devices // REQS
    rows = suffix_kv.shape[0]

    page_paths = [()]
    for step in range(1, steps):
        page_paths = page_paths + [path + (step,) for path in page_paths]
    places = tuple((swapped, path) for path in page_paths for swapped in (False, True))

    first_hop = swap_by_core(suffix_kv, orders, 0)
    mate = swap(suffix_kv, 1)
    own_page, other_page, bias = open_up(devices, orders, places, page_table, hit_tokens, kv_store)
    partner_page = swap(after(other_page, mate), partner)
    mass, shift = attend_first(orders, queries, suffix_kv, mate)
    held = [((), suffix_kv), ((0,), after(first_hop, shift, partner_page))]
    for step in range(1, steps):
        held = held + [(path + (step,), swap_by_core(value, orders, step)) for path, value in held]
    pair = pack([own_page, partner_page])
    pair_hop = swap_by_core(pair, orders, 0)
    page_held = [((), pack([pair, pair_hop]))]
    for step in range(1, steps):
        page_held = page_held + [(path + (step,), swap_by_core(value, orders, step)) for path, value in page_held]

    arrivals, pages = [], {}
    for path, value in held[1:]:
        value = after(value, shift) if len(path) == 2 else value
        arrivals.append([(("block", False, path), value), (("block", True, path), swap(value, 1))])
    home = [(("own",), suffix_kv), (("block", True, ()), mate)]
    if steps == 2 and (2 * rows // devices) % 16 == 0:
        near, across = orders[0], orders[0][0] ^ orders[0][1]
        batches = [(home + arrivals[0] + arrivals[1], (0,) + near), (arrivals[2], (across,))]
    else:
        batches = [(home + sum(arrivals, []), (None,))]
    pieces, spans = [], []
    for batch, hops in batches:
        mine, theirs = pick_for_owners(devices, orders, owner_offset, rows, batch, hops)
        pieces.append((mine, swap(theirs, partner)))
        spans.append(hops)
        if len(pieces) == 1:
            mass, first_sent = after(mass, theirs), theirs
    for n in range(0, len(arrivals) - 1, 2):
        mass = attend_more(orders, queries, shift, mass, sum(arrivals[n : min(n + 2, len(arrivals) - 1)], []))
    for path, value in page_held:
        pages[(False, path)], pages[(True, path)] = value, swap(after(value, first_sent) if path else value, 1)
    attention_out = attend_last(
        orders,
        queries,
        shift,
        mass,
        bias,
        arrivals[-1],
        [pages[place] for place in places],
        home + sum(arrivals[:-1], []),
    )
    return (attention_out, place(devices, pieces, spans, REQS * partner * rows // devices))


def solution(mesh):
    in_specs = (
        P(("groups", "seq"), None),
        P(("groups", "seq"), None),
        P(("groups", "seq"), None, None),
        P("groups", None),
        P("groups"),
        P("groups", None),
    )
    out_specs = (P(("groups", "seq"), None), P(("groups", "seq"), None, None, None))
    return jax.shard_map(shards, mesh=mesh, in_specs=in_specs, out_specs=out_specs, check_vma=False)
```

```python
import functools

import jax
import jax.numpy as jnp
from jax import lax
from jax.experimental import pallas as pl
from jax.experimental.pallas import tpu as pltpu
from jax.sharding import PartitionSpec as P

HD = 128
QH = 32
KVH = 4
REQS = 2
PAGE = 8
SLOTS = 32
GQ = QH // KVH

LOG2E = 1.4426950408889634
OUT_OF_REACH = -1e30
CHUNK = 512
VMEM_BYTES = 16 * 1024 * 1024
OPEN_VMEM_BYTES = 58 * 1024 * 1024
SMALL_VMEM_BYTES = 6 * 1024 * 1024
SAFE_MASS = 1e36
CONTRACT_LAST = (((1,), (1,)), ((), ()))

IN_VMEM = pl.BlockSpec(memory_space=pltpu.VMEM)
IN_SMEM = pl.BlockSpec(memory_space=pltpu.SMEM)
ANYWHERE = pl.BlockSpec(memory_space=pl.ANY)
IN_HBM = pl.BlockSpec(memory_space=pltpu.HBM)


def hop_bits(devices):
    bits = []
    bit = 2
    while bit < devices // REQS:
        bits.append(bit)
        bit *= 2
    return (tuple(bits), tuple(reversed(bits)))


def pick(core, pair):
    return jnp.where(core == 0, pair[0], pair[1])


def swap(value, bit):
    route = [(i, i ^ bit) for i in range(lax.axis_size("seq"))]
    return lax.ppermute(value, "seq", route)


def swap_by_core(value, orders, step):
    route = [(i, i ^ orders[i % 2][step]) for i in range(lax.axis_size("seq"))]
    return lax.ppermute(value, "seq", route)


def after(value, *earlier):
    return lax.optimization_barrier((value,) + earlier)[0]


def source_of(me, swapped, path, orders):
    at = me ^ 1 if swapped else me
    core = at % 2
    for step in path:
        at = at ^ pick(core, (orders[0][step], orders[1][step]))
    return at


def page_bias(me, devices, orders, places, table_ref, hit_ref):
    shape = (4 * PAGE, HD)
    token = lax.broadcasted_iota(jnp.int32, shape, 0)
    slot = token >> (PAGE.bit_length() - 1)
    stores = []
    for swapped, path in places:
        base = source_of(me, swapped, path, orders)
        hop = pick(base & 1, (orders[0][0], orders[1][0]))
        at = jnp.where(slot >= 2, base ^ hop, base)
        stores.append(jnp.where((slot & 1) == 1, at ^ (devices // REQS), at))
    store = jnp.concatenate(stores, axis=0)
    inside = jnp.concatenate([token & (PAGE - 1)] * len(places), axis=0)
    request = me // (devices // REQS)
    position = jnp.zeros_like(store)
    for j in range(table_ref.shape[1]):
        position = jnp.where(store == table_ref[request, j] >> (SLOTS.bit_length() - 1), j * PAGE, position)
    return bias_lanes(jnp.where(position + inside < hit_ref[request], 0.0, OUT_OF_REACH))


def open_kernel(devices, orders, places, table_hbm, hit_hbm, store_ref, *refs):
    own_ref, other_ref, bias_ref, table_ref, hit_ref, sems = refs
    table = pltpu.make_async_copy(table_hbm, table_ref, sems.at[2])
    hits = pltpu.make_async_copy(hit_hbm, hit_ref, sems.at[3])
    table.start()
    hits.start()
    me = lax.axis_index("seq")
    request = me // (devices // REQS)
    copies = []
    table.wait()
    for n, (req, page_ref) in enumerate(((1 - request, other_ref), (request, own_ref))):
        slot = jnp.int32(0)
        for j in range(table_ref.shape[1]):
            away = table_ref[req, j] - me * SLOTS
            slot = jnp.where((away >= 0) & (away < SLOTS), away, slot)
        copies.append(pltpu.make_async_copy(store_ref.at[slot], page_ref, sems.at[n]))
        copies[-1].start()
    hits.wait()
    bias_ref[...] = page_bias(me, devices, orders, places, table_ref, hit_ref)
    for copy in copies:
        copy.wait()


def open_up(devices, orders, places, page_table, hit_tokens, kv_store):
    page = jax.ShapeDtypeStruct(kv_store.shape[1:], kv_store.dtype)
    return pl.pallas_call(
        functools.partial(open_kernel, devices, orders, places),
        out_shape=(
            page,
            page,
            jax.ShapeDtypeStruct((4 * PAGE * len(places), HD), jnp.bfloat16),
        ),
        in_specs=[IN_HBM] * 3,
        out_specs=(IN_VMEM,) * 3,
        scratch_shapes=[
            pltpu.SMEM(page_table.shape, jnp.int32),
            pltpu.SMEM(hit_tokens.shape, jnp.int32),
            pltpu.SemaphoreType.DMA((4,)),
        ],
        compiler_params=pltpu.CompilerParams(vmem_limit_bytes=OPEN_VMEM_BYTES),
        name="open_up",
    )(page_table, hit_tokens, kv_store)


def pack_kernel(*refs):
    refs[-1][...] = jnp.concatenate([ref[...] for ref in refs[:-1]], axis=0)


def pack(pages):
    rows = sum(page.shape[0] for page in pages)
    return pl.pallas_call(
        pack_kernel,
        out_shape=jax.ShapeDtypeStruct((rows, pages[0].shape[1]), pages[0].dtype),
        in_specs=[IN_VMEM] * len(pages),
        out_specs=IN_VMEM,
        compiler_params=pltpu.CompilerParams(vmem_limit_bytes=SMALL_VMEM_BYTES),
        name="pack",
    )(*pages)


def stack(refs, at):
    return jnp.concatenate([ref[first : first + count, at : at + HD] for ref, first, count in refs], axis=0)


def head_rows(q_ref, g):
    heads = range(g * GQ, (g + 1) * GQ)
    return jnp.concatenate([q_ref[:, h * HD : (h + 1) * HD] for h in heads], axis=0)


def with_ones(values):
    return jnp.concatenate([values, jnp.ones_like(values)], axis=1)


def shift_lanes(shift):
    lane = lax.broadcasted_iota(jnp.int32, shift.shape, 1)
    return jnp.where(lane == 0, -shift, jnp.where(lane == 1, 1.0, 0.0)).astype(jnp.bfloat16)


def bias_lanes(bias):
    lane = lax.broadcasted_iota(jnp.int32, bias.shape, 1)
    return jnp.where(lane == 0, 1.0, jnp.where(lane == 1, bias, 0.0)).astype(jnp.bfloat16)


def causal_bias(rows):
    t = lax.broadcasted_iota(jnp.int32, (rows, rows), 0)
    k = lax.broadcasted_iota(jnp.int32, (rows, rows), 1)
    return jnp.where(k <= t, 0.0, OUT_OF_REACH)


SCALE = HD**-0.5 * LOG2E


def first_kernel(orders, q_ref, own_ref, mate_ref, mass_ref, shift_ref):
    me = lax.axis_index("seq")
    rows = q_ref.shape[0]
    mate_bias = jnp.where(me % 2 == 1, 0.0, OUT_OF_REACH)
    bias = jnp.concatenate([causal_bias(rows), jnp.full((rows, rows), mate_bias, jnp.float32)], axis=1)
    refs = ((own_ref, 0, rows), (mate_ref, 0, rows))
    for g in range(KVH):
        at = g * 2 * HD
        scores = lax.dot_general(head_rows(q_ref, g), stack(refs, at), CONTRACT_LAST, preferred_element_type=jnp.float32)
        scores = (scores.reshape(GQ, rows, -1) + bias[None]).reshape(GQ * rows, -1)
        peak = jnp.max(scores, axis=1, keepdims=True)
        shift = jnp.broadcast_to(peak, (GQ * rows, HD)).astype(jnp.bfloat16).astype(jnp.float32)
        weights = jnp.exp2((scores - jnp.concatenate([shift, shift], axis=1)) * SCALE).astype(jnp.bfloat16)
        span = pl.ds(g * GQ * rows, GQ * rows)
        mass_ref[span, :] = jnp.dot(weights, with_ones(stack(refs, at + HD)), preferred_element_type=jnp.float32)
        shift_ref[span, :] = shift_lanes(shift)


def attend_first(orders, queries, own, mate):
    rows = queries.shape[0]
    return pl.pallas_call(
        functools.partial(first_kernel, orders),
        out_shape=(
            jax.ShapeDtypeStruct((QH * rows, 2 * HD), jnp.float32),
            jax.ShapeDtypeStruct((QH * rows, HD), jnp.bfloat16),
        ),
        in_specs=[IN_VMEM] * 3,
        out_specs=(IN_VMEM, IN_VMEM),
        compiler_params=pltpu.CompilerParams(vmem_limit_bytes=VMEM_BYTES),
        cost_estimate=pl.CostEstimate(
            flops=16 * rows * QH * rows * HD, bytes_accessed=4 * rows * QH * HD, transcendentals=2 * rows * QH * rows
        ),
        name="attend_first",
    )(queries, own, mate)


def block_bias(me, orders, kind, rows):
    if kind[0] == "own":
        return bias_lanes(jnp.zeros((rows, HD), jnp.float32))
    source = source_of(me, kind[1], kind[2], orders)
    return bias_lanes(jnp.full((rows, HD), jnp.where(source < me, 0.0, OUT_OF_REACH), jnp.float32))


def add_up(q_wide, group, bias, at):
    keys = jnp.concatenate([stack(group, at), bias], axis=1)
    scores = lax.dot_general(q_wide, keys, CONTRACT_LAST, preferred_element_type=jnp.float32)
    weights = jnp.exp2(scores * SCALE).astype(jnp.bfloat16)
    return jnp.dot(weights, with_ones(stack(group, at + HD)), preferred_element_type=jnp.float32)


def more_kernel(orders, kinds, q_ref, shift_ref, mass_ref, *refs):
    out_ref = refs[-1]
    me = lax.axis_index("seq")
    rows = q_ref.shape[0]
    group = [(ref, 0, rows) for ref in refs[:-1]]
    bias = jnp.concatenate([block_bias(me, orders, kind, rows) for kind in kinds], axis=0)
    for g in range(KVH):
        span = pl.ds(g * GQ * rows, GQ * rows)
        q_wide = jnp.concatenate([head_rows(q_ref, g), shift_ref[span, :]], axis=1)
        out_ref[span, :] = mass_ref[span, :] + add_up(q_wide, group, bias, g * 2 * HD)


def attend_more(orders, queries, shift, mass, batch):
    rows = queries.shape[0]
    keys = rows * len(batch)
    return pl.pallas_call(
        functools.partial(more_kernel, orders, tuple(kind for kind, _ in batch)),
        out_shape=jax.ShapeDtypeStruct(mass.shape, mass.dtype),
        in_specs=[IN_VMEM] * (3 + len(batch)),
        out_specs=IN_VMEM,
        input_output_aliases={2: 0},
        compiler_params=pltpu.CompilerParams(vmem_limit_bytes=VMEM_BYTES),
        cost_estimate=pl.CostEstimate(
            flops=8 * rows * QH * keys * HD, bytes_accessed=4 * rows * QH * HD, transcendentals=rows * QH * keys
        ),
        name="attend_more",
    )(queries, shift, mass, *[value for _, value in batch])


def last_kernel(orders, kinds, page_count, other_kinds, q_ref, shift_ref, mass_ref, bias_ref, *refs):
    me = lax.axis_index("seq")
    rows = q_ref.shape[0]
    block_refs = refs[: len(kinds)]
    page_refs = refs[len(kinds) : len(kinds) + page_count]
    other_refs = refs[len(kinds) + page_count : -9]
    out_ref, kept_ref, wrong_ref, top_ref, denominator_ref, total_ref, block_ref, sems, sem = refs[-9:]
    held = 4 * PAGE
    group = [(ref, 0, rows) for ref in block_refs] + [(ref, 0, held) for ref in page_refs]
    biases = [block_bias(me, orders, kind, rows) for kind in kinds] + [bias_ref[...]]
    bias = jnp.concatenate(biases, axis=0)
    wrong_ref[...] = jnp.zeros_like(wrong_ref)
    width = GQ * HD

    def write(g):
        return pltpu.make_async_copy(kept_ref.at[g], out_ref.at[:, pl.ds(g * width, width)], sems.at[g])

    for g in range(KVH):
        span = pl.ds(g * GQ * rows, GQ * rows)
        q_wide = jnp.concatenate([head_rows(q_ref, g), shift_ref[span, :]], axis=1)
        mass = mass_ref[span, :] + add_up(q_wide, group, bias, g * 2 * HD)
        total, denominator = mass[:, :HD], mass[:, HD:]
        wrong = jnp.where(denominator < SAFE_MASS, 0.0, 1.0)
        wrong_ref[...] = jnp.maximum(wrong_ref[...], jnp.max(wrong.reshape(-1, 8, HD), axis=0))
        attended = (total / denominator).astype(kept_ref.dtype)
        for n in range(GQ):
            kept_ref[g, :, n * HD : (n + 1) * HD] = attended[n * rows : (n + 1) * rows]
        write(g).start()
    for g in range(KVH):
        write(g).wait()

    @pl.when(jnp.max(wrong_ref[...]) > 0.0)
    def _():
        top_ref[...] = jnp.full_like(top_ref, OUT_OF_REACH)
        denominator_ref[...] = jnp.zeros_like(denominator_ref)
        total_ref[...] = jnp.zeros_like(total_ref)
        no_shift = shift_lanes(jnp.zeros((rows, HD), jnp.float32))

        def take(ref, first, count, lanes, causal):
            def one_head(n, carried):
                g, h = n // GQ, n % GQ
                at = pl.multiple_of(g * 2 * HD, 2 * HD)
                span = pl.ds(pl.multiple_of(n * rows, rows), rows)
                q = q_ref[:, pl.ds(pl.multiple_of(n * HD, HD), HD)]
                keys = jnp.concatenate([ref[first : first + count, pl.ds(at, HD)], lanes], axis=1)
                scores = lax.dot_general(
                    jnp.concatenate([q, no_shift], axis=1), keys, CONTRACT_LAST, preferred_element_type=jnp.float32
                )
                if causal:
                    scores = scores + causal_bias(rows)
                top = top_ref[span, :]
                new_top = jnp.maximum(top, jnp.max(scores, axis=1, keepdims=True))
                weights = jnp.exp2((scores - new_top[:, :count]) * SCALE)
                factor = jnp.exp2((top - new_top) * SCALE)
                top_ref[span, :] = new_top
                denominator_ref[span, :] = denominator_ref[span, :] * factor + jnp.sum(weights, axis=1, keepdims=True)
                total_ref[span, :] = total_ref[span, :] * factor + jnp.dot(
                    weights.astype(jnp.bfloat16),
                    ref[first : first + count, pl.ds(at + HD, HD)],
                    preferred_element_type=jnp.float32,
                )
                return carried

            lax.fori_loop(0, QH, one_head, 0)

        for kind, ref in zip(other_kinds, other_refs):
            copy = pltpu.make_async_copy(ref.at[pl.ds(0, rows)], block_ref, sem)
            copy.start()
            copy.wait()
            take(block_ref, 0, rows, block_bias(me, orders, kind, rows), kind[0] == "own")
        for kind, ref in zip(kinds, block_refs):
            take(ref, 0, rows, block_bias(me, orders, kind, rows), False)
        for n, ref in enumerate(page_refs):
            take(ref, 0, held, bias_ref[n * held : (n + 1) * held], False)
        for g in range(KVH):
            for n in range(GQ):
                span = pl.ds((g * GQ + n) * rows, rows)
                attended = total_ref[span, :] / denominator_ref[span, :]
                kept_ref[g, :, n * HD : (n + 1) * HD] = attended.astype(kept_ref.dtype)
            write(g).start()
        for g in range(KVH):
            write(g).wait()


def attend_last(orders, queries, shift, mass, bias, batch, pages, others):
    rows = queries.shape[0]
    keys = rows * len(batch) + bias.shape[0]
    width = 2 * KVH * HD
    return pl.pallas_call(
        functools.partial(
            last_kernel, orders, tuple(kind for kind, _ in batch), len(pages), tuple(kind for kind, _ in others)
        ),
        out_shape=jax.ShapeDtypeStruct((rows, QH * HD), queries.dtype),
        in_specs=[IN_VMEM] * (4 + len(batch) + len(pages)) + [ANYWHERE] * len(others),
        out_specs=ANYWHERE,
        scratch_shapes=[
            pltpu.VMEM((KVH, rows, GQ * HD), queries.dtype),
            pltpu.VMEM((8, HD), jnp.float32),
            *[pltpu.VMEM((QH * rows, HD), jnp.float32)] * 3,
            pltpu.VMEM((rows, width), jnp.bfloat16),
            pltpu.SemaphoreType.DMA((KVH,)),
            pltpu.SemaphoreType.DMA,
        ],
        compiler_params=pltpu.CompilerParams(vmem_limit_bytes=VMEM_BYTES),
        cost_estimate=pl.CostEstimate(
            flops=8 * rows * QH * keys * HD, bytes_accessed=4 * rows * QH * HD, transcendentals=rows * QH * keys
        ),
        name="attend_last",
    )(queries, shift, mass, bias, *[value for _, value in batch], *pages, *[value for _, value in others])


def owner_kernel(devices, orders, rows, kinds, hops, offset_ref, *refs):
    key_refs = refs[: len(kinds)]
    own_ref, other_ref = refs[len(kinds) :]
    me = lax.axis_index("seq")
    group_size = devices // REQS
    request = me // group_size
    each = rows // devices
    kept = own_ref.shape[1]
    lane = lax.broadcasted_iota(jnp.int32, (1, rows), 1)
    row = lax.broadcasted_iota(jnp.int32, (2 * kept, rows), 0)
    wanted_row = jnp.where(row >= kept, row - kept, row)
    residue, landing = lane % devices, lane // devices
    bases = []
    for kind in kinds:
        source = me if kind[0] == "own" else source_of(me, kind[1], kind[2], orders)
        place = source % group_size
        if hops[0] is not None:
            place = source % 2
            for n, hop in enumerate(hops):
                place = place + jnp.where((source ^ me) // 2 == hop // 2, 2 * n, 0)
        bases.append(place * each)
    for g in range(KVH):
        turn = (me - offset_ref[request, g] + devices) % devices
        mine = jnp.where(residue == turn, landing, -kept - rows)
        others = jnp.where(residue == turn ^ (devices // REQS), landing, -kept - rows)
        wanted = jnp.where(row >= kept, others, mine)
        total = jnp.zeros((2 * kept, 2 * HD), jnp.float32)
        for ref, base in zip(key_refs, bases):
            chosen = wanted_row == wanted + base
            total = total + jnp.dot(
                jnp.where(chosen, 1.0, 0.0).astype(jnp.bfloat16),
                ref[:rows, g * 2 * HD : (g + 1) * 2 * HD],
                preferred_element_type=jnp.float32,
            )
        own_ref[g] = total[:kept].astype(own_ref.dtype)
        other_ref[g] = total[kept:].astype(other_ref.dtype)


def pick_for_owners(devices, orders, owner_offset, rows, batch, hops):
    kept = len(batch) * rows // devices
    piece = jax.ShapeDtypeStruct((KVH, kept, 2 * HD), batch[0][1].dtype)
    return pl.pallas_call(
        functools.partial(owner_kernel, devices, orders, rows, tuple(kind for kind, _ in batch), hops),
        out_shape=(piece, piece),
        in_specs=[IN_SMEM] + [IN_VMEM] * len(batch),
        out_specs=(IN_VMEM, IN_VMEM),
        compiler_params=pltpu.CompilerParams(vmem_limit_bytes=SMALL_VMEM_BYTES),
        name="pick_for_owners",
    )(owner_offset, *[value for _, value in batch])


def place_kernel(devices, spans, size, *refs):
    me = lax.axis_index("seq")
    group_size = devices // REQS
    request = me // group_size
    chip = (me % group_size) // 2
    kept = size // REQS
    out_ref = refs[-1]
    for n, hops in enumerate(spans):
        for side, req in enumerate((request, 1 - request)):
            ref = refs[2 * n + side]
            height = ref.shape[1] // len(hops)
            for k, hop in enumerate(hops):
                start = req * kept
                if hop is not None:
                    start = start + (chip ^ (hop // 2)) * height
                rows = pl.ds(pl.multiple_of(start, height), height)
                out_ref[0, :, rows] = ref[:, k * height : (k + 1) * height]


def place(devices, pieces, spans, size):
    flat = [array for pair in pieces for array in pair]
    heads, _, width = flat[0].shape
    return pl.pallas_call(
        functools.partial(place_kernel, devices, tuple(spans), size),
        out_shape=jax.ShapeDtypeStruct((1, heads, size, width), flat[0].dtype),
        in_specs=[IN_VMEM] * len(flat),
        out_specs=IN_VMEM,
        compiler_params=pltpu.CompilerParams(vmem_limit_bytes=SMALL_VMEM_BYTES),
        name="place",
    )(*flat)


def shards(queries, suffix_kv, kv_store, page_table, hit_tokens, owner_offset):
    devices = lax.axis_size("seq")
    orders = hop_bits(devices)
    steps = len(orders[0])
    partner = devices // REQS
    rows = suffix_kv.shape[0]

    page_paths = [()]
    for step in range(1, steps):
        page_paths = page_paths + [path + (step,) for path in page_paths]
    places = tuple((swapped, path) for path in page_paths for swapped in (False, True))

    first_hop = swap_by_core(suffix_kv, orders, 0)
    mate = swap(suffix_kv, 1)
    own_page, other_page, bias = open_up(devices, orders, places, page_table, hit_tokens, kv_store)
    partner_page = swap(after(other_page, mate), partner)
    mass, shift = attend_first(orders, queries, suffix_kv, mate)
    held = [((), suffix_kv), ((0,), after(first_hop, shift, partner_page))]
    for step in range(1, steps):
        held = held + [(path + (step,), swap_by_core(value, orders, step)) for path, value in held]
    pair = pack([own_page, partner_page])
    pair_hop = swap_by_core(pair, orders, 0)

    arrivals, pages = [], {}
    for path, value in held[1:]:
        value = after(value, shift) if len(path) == 2 else value
        arrivals.append([(("block", False, path), value), (("block", True, path), swap(value, 1))])
    home = [(("own",), suffix_kv), (("block", True, ()), mate)]
    if steps == 2 and (2 * rows // devices) % 16 == 0:
        near, across = orders[0], orders[0][0] ^ orders[0][1]
        batches = [(home + arrivals[0] + arrivals[1], (0,) + near), (arrivals[2], (across,))]
    else:
        batches = [(home + sum(arrivals, []), (None,))]
    pieces, spans = [], []
    for batch, hops in batches:
        mine, theirs = pick_for_owners(devices, orders, owner_offset, rows, batch, hops)
        pieces.append((mine, swap(theirs, partner)))
        spans.append(hops)
        if len(pieces) == 1:
            mass, first_sent = after(mass, theirs), theirs
    page_held = [((), pack([pair, after(pair_hop, first_sent)]))]
    for step in range(1, steps):
        page_held = page_held + [(path + (step,), swap_by_core(value, orders, step)) for path, value in page_held]
    for n in range(0, len(arrivals) - 1, 2):
        mass = attend_more(orders, queries, shift, mass, sum(arrivals[n : min(n + 2, len(arrivals) - 1)], []))
    for path, value in page_held:
        pages[(False, path)], pages[(True, path)] = value, swap(after(value, first_sent) if path else value, 1)
    attention_out = attend_last(
        orders,
        queries,
        shift,
        mass,
        bias,
        arrivals[-1],
        [pages[place] for place in places],
        home + sum(arrivals[:-1], []),
    )
    return (attention_out, place(devices, pieces, spans, REQS * partner * rows // devices))


def solution(mesh):
    in_specs = (
        P(("groups", "seq"), None),
        P(("groups", "seq"), None),
        P(("groups", "seq"), None, None),
        P("groups", None),
        P("groups"),
        P("groups", None),
    )
    out_specs = (P(("groups", "seq"), None), P(("groups", "seq"), None, None, None))
    return jax.shard_map(shards, mesh=mesh, in_specs=in_specs, out_specs=out_specs, check_vma=False)
```
